32 devices in a mesh: ctx: 8 (over y, x, core), fsdp: 4 (over z).
Axes of the slice: x: 2, y: 2, z: 4, core: 2. Of those that a mesh axis runs over, the one named last changes fastest.
Arguments:
- inputs: bfloat16 [8, 1024, 1024], P('fsdp', 'ctx'), may hold values from -6 to 6
- time_ids: int32 [8, 1024], P('fsdp', 'ctx'), may hold values from 0 to 511, as said below
- variate_ids: int32 [8, 1024], P('fsdp', 'ctx'), may hold values from 0 to 15, as said below
- seq_lengths: int32 [8], P('fsdp'), may hold values from 256 to 1024, as said below
- w_query: bfloat16 [1024, 1024], P('fsdp'), may hold values from -0.1875 to 0.1875
- w_key: bfloat16 [1024, 1024], P('fsdp'), may hold values from -0.1875 to 0.1875
- w_value: bfloat16 [1024, 1024], P('fsdp'), may hold values from -0.1875 to 0.1875
- w_out: bfloat16 [1024, 1024], P('fsdp'), may hold values from -3 to 3
- w_gate: bfloat16 [1024, 2816], P('fsdp'), may hold values from -0.1875 to 0.1875
- w_up: bfloat16 [1024, 2816], P('fsdp'), may hold values from -0.1875 to 0.1875
- w_down: bfloat16 [2816, 1024], P('fsdp'), may hold values from -0.109375 to 0.109375
- gain_attn: bfloat16 [1024], P('fsdp'), may hold values from 0.5 to 1.5
- gain_ffn: bfloat16 [1024], P('fsdp'), may hold values from 0.5 to 1.5
- head_bias: bfloat16 [16, 2], P('fsdp'), may hold values from -1 to 1
- q_gain: bfloat16 [64], P('fsdp'), may hold values from 0.5 to 1.5
- k_gain: bfloat16 [64], P('fsdp'), may hold values from 0.5 to 1.5
- cotangent: bfloat16 [8, 1024, 1024], P('fsdp', 'ctx'), may hold values from -6 to 6
Outputs:
- output: bfloat16 [8, 1024, 1024], P('fsdp', 'ctx')
- grad_inputs: float32 [8, 1024, 1024], P('fsdp', 'ctx')
- grad_query: float32 [1024, 1024], P('fsdp')
- grad_key: float32 [1024, 1024], P('fsdp')
- grad_value: float32 [1024, 1024], P('fsdp')
- grad_out: float32 [1024, 1024], P('fsdp')
- grad_gate: float32 [1024, 2816], P('fsdp')
- grad_up: float32 [1024, 2816], P('fsdp')
- grad_down: float32 [2816, 1024], P('fsdp')
- grad_gain_attn: float32 [1024], P('fsdp')
- grad_gain_ffn: float32 [1024], P('fsdp')
- grad_bias: float32 [16, 2], P('fsdp')
- grad_q_gain: float32 [64], P('fsdp')
- grad_k_gain: float32 [64], P('fsdp')
The draws below stay inside these ranges and needn't reach their ends.
Inputs may be any that keep to these rules, and one draw needn't show every extreme that they name: `seq_lengths`: in each group of 2 consecutive sequences at least one has all 1024 slots valid. `variate_ids`: within a sequence every variate takes one contiguous run of slots, all runs of the sequence but the last of one length, ids 0, 1, 2, ... in order from slot 0. `time_ids`: A slot's time id is its place within its variate's run.
All inputs are finite; a program needn't handle non-finite values.
Results may differ from the reference program's by a relative error of at most 0.039.
Values may be sent and summed in bfloat16 or wider, within the bound.
No kernel may reach another device: no remote copies, remote signals or barrier semaphores. Data moves between devices by JAX's collectives and lax.ppermute only.
A program may use at most 256 MiB of HBM per device.

```python
import jax
import jax.numpy as jnp
from jax import lax

D = 1024
HEADS = 16
HEAD_DIM = 64
FF = 2816
SLOT_DEV = 128
SEQS = 2
SLOTS = 1024
BATCH = 8


def run_lengths(key):
    drawn = jax.random.randint(key, (BATCH,), SLOT_DEV // 2, 4 * SLOT_DEV + 1)
    index = jnp.arange(BATCH)
    drawn = jnp.where(index == 0, SLOT_DEV // 2, drawn)
    drawn = jnp.where(index == 1, 4 * SLOT_DEV, drawn)
    return drawn[:, None]


def draw_variate_ids(key, part):
    runs = run_lengths(key)
    return (jnp.arange(SLOTS)[None, :] // runs).astype(jnp.int32)


def draw_time_ids(key, part):
    runs = run_lengths(key)
    return (jnp.arange(SLOTS)[None, :] % runs).astype(jnp.int32)


def draw_seq_lengths(key, part):
    key = jax.random.fold_in(key, 13)
    pick_key, length_key = jax.random.split(key)
    groups = BATCH // SEQS
    full_pick = jax.random.randint(pick_key, (groups, 1), 0, SEQS)
    others = jax.random.randint(length_key, (groups, SEQS), SLOTS // 4, SLOTS + 1)
    column = jnp.arange(SEQS)[None, :]
    return jnp.where(column == full_pick, SLOTS, others).reshape(BATCH).astype(jnp.int32)


def steps_of(rng, dims, cuts, low, high):
    loudness, own = 1.0, jax.random.fold_in(rng, 6)
    for dim, parts in cuts:
        steps = jnp.exp(jax.random.uniform(jax.random.fold_in(own, dim), (parts,), jnp.float32, low / len(cuts), high / len(cuts)))
        loudness = loudness * jnp.repeat(steps, dims[dim] // parts).reshape([-1 if axis == dim else 1 for axis in range(len(dims))])
    return loudness


def scatter_about(own_key, extent, deviation, most, shards=(), kind=jnp.bfloat16):
    entries = deviation * jax.random.normal(own_key, extent, jnp.float32)
    if shards:
        entries = entries * steps_of(own_key, extent, shards, -0.22, 0.18)
    return jnp.clip(entries, -most, most).astype(kind)


def setup_inputs(seed: int = 0) -> dict:
    streams_of = jax.random.split(jax.random.key(seed), 18)
    inputs = scatter_about(streams_of[0], (BATCH, SLOTS, D), 1.0, 6.0, ((0, 4), (1, 8)))
    time_ids = draw_time_ids(jax.random.fold_in(streams_of[17], 71), 0)
    variate_ids = draw_variate_ids(jax.random.fold_in(streams_of[17], 71), 0)
    seq_lengths = draw_seq_lengths(jax.random.fold_in(streams_of[17], 71), 0)
    w_query = scatter_about(streams_of[4], (D, D), D ** -0.5, 0.1875, ((0, 4),))
    w_key = scatter_about(streams_of[5], (D, D), D ** -0.5, 0.1875, ((0, 4),))
    w_value = scatter_about(streams_of[6], (D, D), D ** -0.5, 0.1875, ((0, 4),))
    w_out = scatter_about(streams_of[7], (D, D), (max(1, D * 4 // SLOTS)) ** -0.5, 3.0, ((0, 4),))
    w_gate = scatter_about(streams_of[8], (D, FF), D ** -0.5, 0.1875, ((0, 4),))
    w_up = scatter_about(streams_of[9], (D, FF), D ** -0.5, 0.1875, ((0, 4),))
    w_down = scatter_about(streams_of[10], (FF, D), FF ** -0.5, 0.109375, ((0, 4),))
    gain_attn = jnp.clip(1.0 + 0.1 * jax.random.normal(streams_of[11], (D,), jnp.float32), 0.5, 1.5).astype(jnp.bfloat16)
    gain_ffn = jnp.clip(1.0 + 0.1 * jax.random.normal(streams_of[12], (D,), jnp.float32), 0.5, 1.5).astype(jnp.bfloat16)
    head_bias = jnp.clip(jax.random.uniform(streams_of[13], (HEADS, 2), jnp.float32, -1.0, 1.0) * steps_of(streams_of[13], (HEADS, 2), ((0, 4),), -0.4, 0.0), -1.0, 1.0).astype(jnp.bfloat16)
    q_gain = jnp.clip(1.0 + 0.1 * jax.random.normal(streams_of[14], (HEAD_DIM,), jnp.float32), 0.5, 1.5).astype(jnp.bfloat16)
    k_gain = jnp.clip(1.0 + 0.1 * jax.random.normal(streams_of[15], (HEAD_DIM,), jnp.float32), 0.5, 1.5).astype(jnp.bfloat16)
    cotangent = scatter_about(streams_of[16], (BATCH, SLOTS, D), 1.0, 6.0, ((0, 4), (1, 8)))
    return dict(inputs=inputs, time_ids=time_ids, variate_ids=variate_ids, seq_lengths=seq_lengths, w_query=w_query, w_key=w_key, w_value=w_value, w_out=w_out, w_gate=w_gate, w_up=w_up, w_down=w_down, gain_attn=gain_attn, gain_ffn=gain_ffn, head_bias=head_bias, q_gain=q_gain, k_gain=k_gain, cotangent=cotangent)


EPSILON = 1e-05
ROPE_BASE = 10000.0
NEG_FILL = -1e+30
PRECISE = lax.Precision.HIGHEST

@jax.custom_vjp
def low(v):
    return lax.optimization_barrier(v.astype(jnp.bfloat16)).astype(jnp.float32)

@jax.custom_vjp
def low_back(v):
    return v

def low_keep(v):
    return (low(v), None)

def low_pass(kept, grad):
    return (grad,)

def back_keep(v):
    return (v, None)

def back_low(kept, grad):
    return (low(grad),)
low.defvjp(low_keep, low_pass)
low_back.defvjp(back_keep, back_low)

def matmul_hi(left, right):
    return jnp.dot(left, right, precision=PRECISE)

def rms_unit(vector):
    return vector * lax.rsqrt(lax.optimization_barrier(jnp.mean(vector * vector, axis=-1, keepdims=True)) + EPSILON)

def rope_pair(time_ids):
    half_dim = HEAD_DIM // 2
    frequency = ROPE_BASE ** (-jnp.arange(half_dim).astype(jnp.float32) * (2.0 / HEAD_DIM))
    angles = time_ids.astype(jnp.float32)[:, None] * frequency
    return (jnp.cos(angles)[:, None, :], jnp.sin(angles)[:, None, :])

def rotate(vector, cosine, sine_part):
    half_dim = vector.shape[-1] // 2
    front_half = vector[..., :half_dim]
    back_half = vector[..., half_dim:]
    return jnp.concatenate([front_half * cosine - back_half * sine_part, back_half * cosine + front_half * sine_part], axis=-1)

def one_sequence(resid_in, time_ids, variate_ids, seq_length, params):
    w_query, w_key, w_value, w_out, w_gate, w_up, w_down, gain_attn, gain_ffn, head_bias, q_gain, k_gain = params
    num_slots = resid_in.shape[0]
    is_valid = jnp.arange(num_slots) < seq_length
    normed1 = low(rms_unit(resid_in) * gain_attn)
    query_pre = low_back(matmul_hi(normed1, w_query)).reshape(num_slots, HEADS, HEAD_DIM)
    key_pre = low_back(matmul_hi(normed1, w_key)).reshape(num_slots, HEADS, HEAD_DIM)
    value_low = low(low_back(matmul_hi(normed1, w_value))).reshape(num_slots, HEADS, HEAD_DIM)
    query_normed = rms_unit(query_pre) * q_gain
    key_normed = rms_unit(key_pre) * k_gain
    cosine, sine_part = rope_pair(time_ids)
    query_rot = low(rotate(query_normed, cosine, sine_part))
    key_rot = low(rotate(key_normed, cosine, sine_part))
    block_rows = 512 if num_slots % 512 == 0 else num_slots
    num_blocks = num_slots // block_rows

    def attend(packed):
        query_blk, vid_blk = packed
        scores = jnp.einsum('qhd,khd->hqk', query_blk, key_rot, precision=PRECISE) * HEAD_DIM ** (-0.5)
        same_var = (vid_blk[:, None] == variate_ids[None, :])[None]
        scores = scores + jnp.where(same_var, head_bias[:, 0][:, None, None], head_bias[:, 1][:, None, None])
        scores = low_back(scores)
        scores = jnp.where(is_valid[None, None, :], scores, NEG_FILL)
        row_top = lax.optimization_barrier(jnp.max(scores, axis=-1, keepdims=True))
        exp_terms = jnp.where(is_valid[None, None, :], jnp.exp(scores - row_top), 0.0)
        attn_prob = exp_terms / lax.optimization_barrier(jnp.sum(exp_terms, axis=-1, keepdims=True))
        return jnp.einsum('hqk,khd->qhd', low(attn_prob), value_low, precision=PRECISE)
    mixed_out = lax.map(jax.checkpoint(attend), (query_rot.reshape(num_blocks, block_rows, HEADS, HEAD_DIM), variate_ids.reshape(num_blocks, block_rows)))
    attn_in = low(low_back(mixed_out.reshape(num_slots, D)))
    hidden_state = resid_in + low_back(matmul_hi(attn_in, w_out))
    normed2 = low(rms_unit(hidden_state) * gain_ffn)
    gate_pre = low_back(matmul_hi(normed2, w_gate))
    up_pre = low_back(matmul_hi(normed2, w_up))
    inner_act = low(jax.nn.silu(gate_pre) * up_pre)
    result = hidden_state + matmul_hi(inner_act, w_down)
    return result * is_valid[:, None].astype(result.dtype)

def reference(inputs, time_ids, variate_ids, seq_lengths, w_query, w_key, w_value, w_out, w_gate, w_up, w_down, gain_attn, gain_ffn, head_bias, q_gain, k_gain, cotangent):
    params = tuple((weight.astype(jnp.float32) for weight in (w_query, w_key, w_value, w_out, w_gate, w_up, w_down, gain_attn, gain_ffn, head_bias, q_gain, k_gain)))

    def forward(inputs_f, params_f):

        def per_sequence(packed):
            return one_sequence(packed[0], packed[1], packed[2], packed[3], params_f)
        return lax.map(jax.checkpoint(per_sequence), (inputs_f, time_ids, variate_ids, seq_lengths))
    result, pullback = jax.vjp(forward, inputs.astype(jnp.float32), params)
    grad_inputs, grads = pullback(cotangent.astype(jnp.float32))
    return (result.astype(jnp.bfloat16), grad_inputs, grads[0], grads[1], grads[2], grads[3], grads[4], grads[5], grads[6], grads[7], grads[8], grads[9], grads[10], grads[11])
```

```python
import functools

import jax
import jax.numpy as jnp
from jax import lax
from jax.experimental import pallas as pl
from jax.experimental.pallas import tpu as pltpu
from jax.sharding import PartitionSpec as P

EPSILON = 1e-05
ROPE_BASE = 10000.0
NEG_FILL = -1e30
HEAD_DIM = 64
VARIATES = 64
BF = jnp.bfloat16
F32 = jnp.float32
PAD = 16

NT = (((1,), (1,)), ((), ()))
TN = (((0,), (0,)), ((), ()))
NN = (((1,), (0,)), ((), ()))


def mm(left, right, dims=NN):
    return lax.dot_general(left, right, dims, preferred_element_type=F32)


def kernel_call(kernel, out_shapes, *operands, scalars=None, scratch=(), flops=0):
    specs = [pl.BlockSpec(memory_space=pltpu.VMEM)] * len(operands)
    if scalars is not None:
        specs = [pl.BlockSpec(memory_space=pltpu.SMEM)] + specs
        operands = (scalars,) + operands
    moved = sum(o.size * o.dtype.itemsize for o in operands)
    moved += sum(o.size * jnp.dtype(o.dtype).itemsize for o in out_shapes)
    return pl.pallas_call(
        kernel,
        out_shape=out_shapes,
        in_specs=specs,
        out_specs=[pl.BlockSpec(memory_space=pltpu.VMEM)] * len(out_shapes),
        scratch_shapes=list(scratch),
        cost_estimate=pl.CostEstimate(flops=flops, bytes_accessed=moved, transcendentals=0),
        compiler_params=pltpu.CompilerParams(vmem_limit_bytes=48 * 2**20),
    )(*operands)


def shape_of(dims, dtype):
    return jax.ShapeDtypeStruct(tuple(dims), dtype)


def assemble(pieces, places, dims):
    rows, cols = pieces[0].shape
    if rows % 16 or cols % 128:
        whole = jnp.zeros(dims, BF)
        for piece, (row, col) in zip(pieces, places):
            whole = lax.dynamic_update_slice(whole, piece, (row, col))
        return whole
    flat = jnp.stack([jnp.asarray(v, jnp.int32) for place in places for v in place])

    def kernel(index, *refs):
        out = refs[-1]
        for n, ref in enumerate(refs[:-1]):
            row = pl.multiple_of(index[2 * n], 16)
            col = pl.multiple_of(index[2 * n + 1], 128)
            out[pl.ds(row, rows), pl.ds(col, cols)] = ref[...]

    return kernel_call(kernel, [shape_of(dims, BF)], *pieces, scalars=flat)[0]


def head_sum(values):
    row = lax.broadcasted_iota(jnp.int32, (128, 128), 0) // HEAD_DIM
    col = lax.broadcasted_iota(jnp.int32, (128, 128), 1) // HEAD_DIM
    ones = (row == col).astype(BF)
    high = values.astype(BF)
    low = (values - high.astype(F32)).astype(BF)
    return mm(high, ones) + mm(low, ones)


def half_swap(values):
    lane = lax.broadcasted_iota(jnp.int32, values.shape, 1)
    return jnp.where(
        lane % HEAD_DIM < HEAD_DIM // 2, pltpu.roll(values, 96, 1), pltpu.roll(values, 32, 1)
    )


def qkv_kernel(slots, width, xa, xb, w, gain, q_gain, k_gain, cosine, sine, qr, kr, vr, qp, kp, n1):
    for half, ref in enumerate((xa, xb)):
        x = ref[pl.ds(0, slots), :].astype(F32)
        scale = lax.rsqrt(jnp.mean(x * x, axis=-1, keepdims=True) + EPSILON)
        n1[pl.ds(half * slots, slots), :] = (x * scale * gain[...]).astype(BF)
    pre = mm(n1[...], w[...])
    vr[...] = pre[:, 2 * width :].astype(BF)
    qp[...] = pre[:, :width]
    kp[...] = pre[:, width : 2 * width]
    for source, head_gain, target in ((qp, q_gain, qr), (kp, k_gain, kr)):
        for g in range(width // 128):
            lanes = pl.ds(128 * g, 128)
            value = source[:, lanes]
            scale = lax.rsqrt(head_sum(value * value) * (1.0 / HEAD_DIM) + EPSILON)
            normed = value * scale * head_gain[:, lanes]
            target[:, lanes] = (normed * cosine[...] + half_swap(normed) * sine[...]).astype(BF)


def key_features(kind, bias, h):
    kind = kind.astype(F32)
    same, other = bias[2 * h], bias[2 * h + 1]
    return jnp.where(kind == 0.0, other, jnp.where(kind == 1.0, same, NEG_FILL)).astype(BF)


def attend_kernel(heads, chunks, bias, kind, k, v, *refs):
    queries, hots = refs[:chunks], refs[chunks : 2 * chunks]
    mixes, lows = refs[2 * chunks : 3 * chunks], refs[3 * chunks :]
    for h in range(heads):
        lanes = pl.ds(HEAD_DIM * h, HEAD_DIM)
        keys = jnp.concatenate([k[:, lanes], key_features(kind[...], bias, h)], axis=1)
        values = v[:, lanes]
        for c in range(chunks):
            query = jnp.concatenate([queries[c][:, lanes] * BF(0.125), hots[c][...]], axis=1)
            terms = jnp.exp(mm(query, keys, NT))
            denom = jnp.sum(terms, axis=-1, keepdims=True)
            mix = mm(terms.astype(BF), values) / denom
            mixes[c][:, lanes] = mix
            lows[c][:, lanes] = mix.astype(BF)


def mix_out_kernel(width, parts, scalars, xa, xb, w_out, gain, *refs):
    pieces, (h_ref, n2) = refs[:parts], refs[parts:]
    slots = h_ref.shape[0] // 2
    total = None
    for d in range(parts):
        row = pl.multiple_of(scalars[d] * width, 128)
        term = mm(pieces[d][...], w_out[pl.ds(row, width), :])
        total = term if total is None else total + term
    own = jnp.concatenate([xa[pl.ds(0, slots), :], xb[pl.ds(0, slots), :]], axis=0)
    h = own.astype(F32) + total
    h_ref[...] = h
    scale = lax.rsqrt(jnp.mean(h * h, axis=-1, keepdims=True) + EPSILON)
    n2[...] = (h * scale * gain[...]).astype(BF)


def ffn_kernel(width, n2, dy, w_gu, w_down, y, dn2, act, dgu):
    pre = mm(n2[...], w_gu[...])
    gate, up = pre[:, :width], pre[:, width:]
    sig = jax.nn.sigmoid(gate)
    silu = gate * sig
    low = (silu * up).astype(BF)
    act[...] = low
    y[...] = mm(low, w_down[...]).astype(BF)
    d_act = mm(dy[...], w_down[...], NT)
    d_up = (d_act * silu).astype(BF)
    d_gate = (d_act * up * sig * (1.0 + gate * (1.0 - sig))).astype(BF)
    both = jnp.concatenate([d_gate, d_up], axis=1)
    dgu[...] = both
    dn2[...] = mm(both, w_gu[...], NT).astype(BF)


def norm_back(grad, x, gain):
    scale = lax.rsqrt(jnp.mean(x * x, axis=-1, keepdims=True) + EPSILON)
    unit = x * scale
    scaled = grad * gain
    return scale * (scaled - unit * jnp.mean(scaled * unit, axis=-1, keepdims=True))


def hidden_back_kernel(width, parts, scalars, h, dy, gain, w_out, *refs):
    terms, (d_h, d_low), d_mix = refs[:parts], refs[parts : parts + 2], refs[parts + 2 :]
    grad = terms[0][...].astype(F32)
    for ref in terms[1:]:
        grad = grad + ref[...].astype(F32)
    total = dy[...].astype(F32) + norm_back(grad, h[...], gain[...])
    d_h[...] = total
    low = total.astype(BF)
    d_low[...] = low
    for d in range(parts):
        row = pl.multiple_of(scalars[d] * width, 128)
        d_mix[d][...] = mm(low, w_out[pl.ds(row, width), :], NT).astype(BF)


def input_back_kernel(parts, xa, xb, d_h, gain, *refs):
    terms, (out, low) = refs[:parts], refs[parts:]
    slots = out.shape[0]
    grad = terms[0][...].astype(F32)
    for ref in terms[1:]:
        grad = grad + ref[...].astype(F32)
    own = jnp.concatenate([xa[pl.ds(0, slots), :], xb[pl.ds(0, slots), :]], axis=0).astype(F32)
    total = d_h[...] + norm_back(grad, own, gain[...])
    out[...] = total[:slots]
    low[...] = total[slots:].astype(BF)


def attend_back_kernel(
    heads, chunks, bias, kind, hot, q, k, v, dmix, mix, qp, kp, q_gain, k_gain, cosine, sine,
    d_qkv, bias_out, gains_out, dq_scr, dk_scr, dv_scr,
):
    slots, width = k.shape
    rows = slots // chunks
    dk_scr[...] = jnp.zeros_like(dk_scr)
    dv_scr[...] = jnp.zeros_like(dv_scr)
    bias_out[...] = jnp.zeros_like(bias_out)
    gains_out[...] = jnp.zeros_like(gains_out)
    key_hot = hot[...]

    def chunk(c, carry):
        part = pl.ds(pl.multiple_of(c * rows, rows), rows)
        query_hot = hot[part, :]
        for h in range(heads):
            lanes = pl.ds(HEAD_DIM * h, HEAD_DIM)
            key = k[:, lanes]
            keys = jnp.concatenate([key, key_features(kind[...], bias, h)], axis=1)
            query = q[part, lanes] * BF(0.125)
            grad = dmix[part, lanes]
            product = mix[part, lanes] * grad.astype(F32)
            high = product.astype(BF)
            low = (product - high.astype(F32)).astype(BF)
            ones = jnp.ones((8, HEAD_DIM), BF)
            delta = (mm(ones, high, NT) + mm(ones, low, NT))[:1]
            terms = jnp.exp(mm(keys, jnp.concatenate([query, query_hot], axis=1), NT))
            prob = terms * (1.0 / jnp.sum(terms, axis=0, keepdims=True))
            d_score = (prob * (mm(v[:, lanes], grad, NT) - delta)).astype(BF)
            dk_scr[:, lanes] += mm(d_score, query)
            dv_scr[:, lanes] += mm(prob.astype(BF), grad)
            both = mm(d_score, jnp.concatenate([key, key_hot], axis=1), TN)
            dq_scr[part, lanes] = both[:, :HEAD_DIM] * 0.125
            pairs = both[:, HEAD_DIM:]
            hot_f = query_hot.astype(F32)
            same = jnp.sum(pairs * hot_f, axis=0, keepdims=True)
            other = jnp.sum(pairs * (1.0 - hot_f), axis=0, keepdims=True)
            bias_out[pl.ds(2 * h, 1), :] += jnp.concatenate([same, same], axis=1)
            bias_out[pl.ds(2 * h + 1, 1), :] += jnp.concatenate([other, other], axis=1)
        return carry

    lax.fori_loop(0, chunks, chunk, 0)

    def finish(c, carry):
        part = pl.ds(pl.multiple_of(c * rows, rows), rows)
        cos_part, sin_part = cosine[part, :], sine[part, :]
        for n, (grads, pre, gain) in enumerate(((dq_scr, qp, q_gain), (dk_scr, kp, k_gain))):
            for g in range(width // 128):
                lanes = pl.ds(128 * g, 128)
                grad = grads[part, lanes]
                value = pre[part, lanes]
                scale = lax.rsqrt(head_sum(value * value) * (1.0 / HEAD_DIM) + EPSILON)
                unit = value * scale
                d_normed = grad * cos_part - half_swap(grad) * sin_part
                gains_out[pl.ds(n, 1), :] += jnp.sum(d_normed * unit, axis=0, keepdims=True)
                scaled = d_normed * gain[:, lanes]
                mean = head_sum(scaled * unit) * (1.0 / HEAD_DIM)
                d_qkv[part, pl.ds(n * width + 128 * g, 128)] = (
                    scale * (scaled - unit * mean)
                ).astype(BF)
        d_qkv[part, pl.ds(2 * width, width)] = dv_scr[part, :].astype(BF)
        return carry

    lax.fori_loop(0, chunks, finish, 0)


def layer(
    ctx, fsdp, inputs, time_ids, variate_ids, seq_lengths, w_query, w_key, w_value, w_out, w_gate,
    w_up, w_down, gain_attn, gain_ffn, head_bias, q_gain, k_gain, cotangent,
):
    chips = ctx // 2
    _, slots, model = inputs.shape
    heads = model // HEAD_DIM // chips
    width = heads * HEAD_DIM
    rows_z = w_query.shape[0]
    half_z = rows_z // 2
    hidden = w_gate.shape[1]
    ff = hidden // chips
    ff_z = ff // fsdp
    chunk = 2 * slots
    span = chips * chunk
    here = lax.axis_index("ctx")
    depth = lax.axis_index("fsdp")
    core, chip = here % 2, here // 2

    def px(a, p):
        return lax.ppermute(a, "ctx", [(n, n ^ p) for n in range(ctx)])

    def pz(a, p):
        return lax.ppermute(a, "fsdp", [(n, n ^ p) for n in range(fsdp)])

    def gather_blocks(own, other):
        got = [own] + [px(other if p % 2 else own, p) for p in range(1, min(ctx, 6))]
        if ctx == 8:
            return got + [px(got[2], 4), px(got[5], 2)]
        return got + [px(other if p % 2 else own, p) for p in range(6, ctx)]

    def gather_chips(own):
        if chips == 4:
            cut = own.shape[0] // 2
            side, up = px(own, 2), px(own, 4)
            corner = jnp.concatenate([px(side[:cut], 4), px(up[cut:], 2)], axis=0)
            return [own, side, up, corner]
        return [own] + [px(own, 2 * d) for d in range(1, chips)]

    def exchange(parts):
        return [parts[0]] + [px(parts[d], 2 * d) for d in range(1, chips)]

    def mine(pair):
        return lax.dynamic_index_in_dim(pair, core, 0, keepdims=False)

    def theirs(pair):
        return lax.dynamic_index_in_dim(pair, 1 - core, 0, keepdims=False)

    ids = jnp.stack([time_ids >> 8, time_ids & 255, variate_ids], axis=1).astype(BF)
    ids = jnp.pad(ids, ((0, 0), (0, PAD - 3), (0, model - slots)))
    message = jnp.concatenate([inputs, ids], axis=1)
    blocks = gather_blocks(mine(message), theirs(message))

    def columns(w, at, count):
        return lax.dynamic_slice_in_dim(w, at, count, 1)

    small = jnp.concatenate(
        [gain_attn, gain_ffn, head_bias[:, 0], head_bias[:, 1], q_gain, k_gain]
    )
    small = jnp.pad(small[None], ((0, PAD - 1), (0, 3 * width - small.shape[0])))
    qkv_cols = jnp.concatenate([columns(w, chip * width, width) for w in (w_query, w_key, w_value)], 1)
    qkv_halves = qkv_cols.reshape(2, half_z, 3 * width)
    own_qkv = jnp.concatenate([mine(qkv_halves), small], axis=0)
    got_qkv = [own_qkv] + [pz(own_qkv, p) for p in range(1, fsdp)]
    swapped_qkv = [theirs(qkv_halves)] + [px(a[:half_z], 1) for a in got_qkv[1:]]

    def z_rows(count, p, c):
        return (depth ^ p) * 2 * count + (core ^ c) * count

    w_qkv = assemble(
        [a[:half_z] for a in got_qkv] + swapped_qkv,
        [(z_rows(half_z, p, c), 0) for c in range(2) for p in range(fsdp)],
        (model, 3 * width),
    )
    smalls = jnp.stack([a[half_z] for a in got_qkv])
    smalls = smalls[depth ^ jnp.arange(fsdp)]
    heads_z = head_bias.shape[0]
    dims_z = q_gain.shape[0]
    cuts = [0, rows_z, 2 * rows_z]
    cuts += [cuts[-1] + heads_z, cuts[-1] + 2 * heads_z]
    cuts += [cuts[-1] + dims_z, cuts[-1] + 2 * dims_z]
    gain1, gain2, bias0, bias1, gain_q, gain_k = (
        smalls[:, a:b].reshape(-1).astype(F32) for a, b in zip(cuts[:-1], cuts[1:])
    )
    gain1_row, gain2_row = gain1[None], gain2[None]
    q_row, k_row = jnp.tile(gain_q, heads)[None], jnp.tile(gain_k, heads)[None]
    bias = lax.dynamic_slice_in_dim(jnp.stack([bias0, bias1], 1), chip * heads, heads, 0).reshape(-1)

    piece = rows_z // ctx
    own_out = lax.dynamic_slice_in_dim(w_out, here * piece, piece, 0)
    z_out = jnp.concatenate([own_out] + [pz(own_out, p) for p in range(1, fsdp)], axis=0)
    chips_out = gather_chips(z_out)
    cores_out = px(jnp.concatenate(chips_out, axis=0), 1)
    out_pieces, out_places = [], []
    for c in range(2):
        for d in range(chips):
            for p in range(fsdp):
                n = d * fsdp + p
                source = chips_out[d] if c == 0 else cores_out[d * fsdp * piece : (d + 1) * fsdp * piece]
                out_pieces.append(source[p * piece : (p + 1) * piece])
                out_places.append(((depth ^ p) * rows_z + (here ^ (2 * d + c)) * piece, 0))
    w_o = assemble(out_pieces, out_places, (model, model))

    def ff_cols(w):
        return jnp.concatenate(
            [columns(w, n * (hidden // fsdp) + chip * ff_z, ff_z) for n in range(fsdp)], 1
        )

    gu_halves = jnp.concatenate([ff_cols(w_gate), ff_cols(w_up)], 1).reshape(2, half_z, 2 * ff)
    own_gu = mine(gu_halves)
    got_gu = [own_gu] + [pz(own_gu, p) for p in range(1, fsdp)]
    swapped_gu = [theirs(gu_halves)] + [px(a, 1) for a in got_gu[1:]]
    w_gu = assemble(
        got_gu + swapped_gu,
        [(z_rows(half_z, p, c), 0) for c in range(2) for p in range(fsdp)],
        (model, 2 * ff),
    )
    down_rows = lax.dynamic_slice_in_dim(w_down, chip * ff_z, ff_z, 0)
    half_m = model // 2
    own_down = columns(down_rows, core * half_m, half_m)
    got_down = [own_down] + [pz(own_down, p) for p in range(1, fsdp)]
    swapped_down = [columns(down_rows, (1 - core) * half_m, half_m)] + [px(a, 1) for a in got_down[1:]]
    w_d = assemble(
        got_down + swapped_down,
        [((depth ^ p) * ff_z, (core ^ c) * half_m) for c in range(2) for p in range(fsdp)],
        (ff, model),
    )

    length = lax.dynamic_index_in_dim(seq_lengths, core, 0, keepdims=False)
    half = HEAD_DIM // 2
    frequency = ROPE_BASE ** (-(jnp.arange(128) % half).astype(F32) * (2.0 / HEAD_DIM))
    sign = jnp.where(jnp.arange(128) % HEAD_DIM < half, -1.0, 1.0)
    tables = []
    for d in range(chips):
        rows = jnp.concatenate([blocks[2 * d][slots : slots + 3, :slots], blocks[2 * d + 1][slots : slots + 3, :slots]], axis=1).astype(F32)
        angles = (rows[0] * 256.0 + rows[1])[:, None] * frequency
        same = rows[2][:, None] == jnp.arange(VARIATES).astype(F32)
        position = jnp.concatenate([(here ^ (2 * d + c)) * slots + jnp.arange(slots) for c in range(2)])
        valid = (position < length)[:, None]
        kind = jnp.where(valid, same.astype(F32), 2.0).astype(BF)
        tables.append((jnp.cos(angles), jnp.sin(angles) * sign, same.astype(BF), kind, valid))

    parts = []
    for d in range(chips):
        parts.append(
            kernel_call(
                functools.partial(qkv_kernel, slots, width),
                [shape_of((chunk, width), BF)] * 3 + [shape_of((chunk, width), F32)] * 2 + [shape_of((chunk, model), BF)],
                blocks[2 * d], blocks[2 * d + 1], w_qkv, gain1_row, q_row, k_row, tables[d][0], tables[d][1],
                flops=2 * chunk * model * 3 * width,
            )
        )

    def joined(n):
        return jnp.concatenate([a[n] for a in parts], axis=0)

    k_all, v_all = joined(1), joined(2)
    kinds = jnp.concatenate([a[3] for a in tables], axis=0)
    hots = jnp.concatenate([a[2] for a in tables], axis=0)
    outs = kernel_call(
        functools.partial(attend_kernel, heads, chips),
        [shape_of((chunk, width), F32)] * chips + [shape_of((chunk, width), BF)] * chips,
        kinds, k_all, v_all, *[a[0] for a in parts], *[a[2] for a in tables],
        scalars=bias, flops=4 * span * span * width,
    )
    mixes, mix_low = outs[:chips], outs[chips:]

    chip_of = jnp.stack([chip ^ d for d in range(chips)]).astype(jnp.int32)
    mix_got = exchange(mix_low)
    hidden_state, normed2 = kernel_call(
        functools.partial(mix_out_kernel, width, chips),
        [shape_of((chunk, model), F32), shape_of((chunk, model), BF)],
        blocks[0], blocks[1], w_o, gain2_row, *mix_got,
        scalars=chip_of, flops=2 * chunk * model * model,
    )

    dy_blocks = gather_blocks(mine(cotangent), theirs(cotangent))
    dys = []
    for d in range(chips):
        dy = jnp.concatenate([dy_blocks[2 * d], dy_blocks[2 * d + 1]], axis=0)
        dys.append(jnp.where(tables[d][4], dy, BF(0)))
    n2_got = gather_chips(normed2)
    ffn = []
    for d in range(chips):
        ffn.append(
            kernel_call(
                functools.partial(ffn_kernel, ff),
                [shape_of((chunk, model), BF)] * 2 + [shape_of((chunk, ff), BF), shape_of((chunk, 2 * ff), BF)],
                n2_got[d], dys[d], w_gu, w_d,
                flops=2 * chunk * model * ff * 6,
            )
        )
    dn2_got = exchange([a[1] for a in ffn])
    outs = kernel_call(
        functools.partial(hidden_back_kernel, width, chips),
        [shape_of((chunk, model), F32), shape_of((chunk, model), BF)] + [shape_of((chunk, width), BF)] * chips,
        hidden_state, dys[0], gain2_row, w_o, *dn2_got,
        scalars=chip_of, flops=2 * chunk * model * model,
    )
    d_hidden, d_hidden_low = outs[:2]
    dmix_got = exchange(outs[2:])

    n2_all = jnp.concatenate(n2_got, axis=0)
    dy_all = jnp.concatenate(dys, axis=0)
    act_all = jnp.concatenate([a[2] for a in ffn], axis=0)
    dgu_all = jnp.concatenate([a[3] for a in ffn], axis=0)
    grad_gu = mm(n2_all, dgu_all, TN)
    grad_d = mm(act_all, dy_all, TN)
    gain2_part = jnp.sum(grad_gu * w_gu.astype(F32), axis=1) / gain2

    def z_sum(summed):
        total = lax.dynamic_index_in_dim(summed, depth, 0, keepdims=False).astype(F32)
        for p in range(1, fsdp):
            total = total + pz(lax.dynamic_index_in_dim(summed, depth ^ p, 0, keepdims=False), p).astype(F32)
        return total

    def core_sum(halves):
        own = lax.dynamic_index_in_dim(halves, core, 1, keepdims=False)
        other = lax.dynamic_index_in_dim(halves, 1 - core, 1, keepdims=False)
        return (own.astype(F32) + px(other.astype(BF), 1).astype(F32)).astype(BF)

    def all_pieces(own):
        same = gather_chips(own)
        both = jnp.stack(same)
        other = px(both, 1)
        pairs = jnp.where(core == 0, jnp.stack([both, other], 1), jnp.stack([other, both], 1))
        return pairs[chip ^ jnp.arange(chips)]

    gu_z = z_sum(core_sum(grad_gu.reshape(fsdp, 2, half_z, 2 * ff))).astype(BF)
    gu_all = all_pieces(gu_z).reshape(chips, rows_z, 2, fsdp, ff_z)
    total_gu = gu_all.transpose(2, 1, 3, 0, 4).reshape(2, rows_z, hidden).astype(F32)
    d_z = z_sum(core_sum(grad_d.reshape(fsdp, ff_z, 2, half_m).transpose(0, 2, 1, 3))).astype(BF)
    total_d = all_pieces(d_z).transpose(0, 2, 1, 3).reshape(hidden // fsdp, model).astype(F32)

    y_got = exchange([a[0] for a in ffn])
    result = hidden_state
    for part in y_got:
        result = result + part.astype(F32)
    result = jnp.where(tables[0][4], result, 0.0).astype(BF)

    def by_sequence(own, other):
        return jnp.where(core == 0, jnp.stack([own, other]), jnp.stack([other, own]))

    output = by_sequence(result[:slots], px(result[slots:], 1))

    mix_abs = jnp.stack(mix_got)[chip ^ jnp.arange(chips)]
    grad_o = mm(mix_abs.transpose(1, 0, 2).reshape(chunk, model), d_hidden_low, TN)
    grad_o = core_sum(grad_o.reshape(fsdp, 2, half_z, model))
    o_parts = grad_o.reshape(fsdp, chips, half_z // chips, model).transpose(1, 0, 2, 3)
    o_got = exchange([lax.dynamic_index_in_dim(o_parts, chip ^ d, 0, keepdims=False) for d in range(chips)])
    o_sum = o_got[0].astype(F32)
    for part in o_got[1:]:
        o_sum = o_sum + part.astype(F32)
    o_z = z_sum(o_sum.astype(BF)).astype(BF)
    total_o = all_pieces(o_z).transpose(1, 0, 2, 3).reshape(rows_z, model).astype(F32)

    d_qkv, bias_rows, gain_rows = kernel_call(
        functools.partial(attend_back_kernel, heads, chips),
        [shape_of((span, 3 * width), BF), shape_of((max(8, 2 * heads), 128), F32), shape_of((8, 128), F32)],
        kinds, hots, joined(0), k_all, v_all, jnp.concatenate(dmix_got, axis=0),
        jnp.concatenate(mixes, axis=0), joined(3), joined(4), q_row, k_row,
        jnp.concatenate([a[0] for a in tables], axis=0), jnp.concatenate([a[1] for a in tables], axis=0),
        scalars=bias, flops=10 * span * span * width,
        scratch=[pltpu.VMEM((span, width), F32)] * 3,
    )
    n1_all = joined(5)
    d_n1 = mm(d_qkv, w_qkv, NT).astype(BF).reshape(chips, chunk, model)
    dn1_got = exchange([d_n1[d] for d in range(chips)])
    own_grad, their_grad = kernel_call(
        functools.partial(input_back_kernel, chips),
        [shape_of((slots, model), F32), shape_of((slots, model), BF)],
        blocks[0], blocks[1], d_hidden, gain1_row, *dn1_got,
    )
    grad_inputs = by_sequence(own_grad, px(their_grad, 1).astype(F32))

    grad_qkv = mm(n1_all, d_qkv, TN)
    gain1_part = jnp.sum(grad_qkv * w_qkv.astype(F32), axis=1) / gain1
    bias_part = jnp.sum(bias_rows[: 2 * heads, :HEAD_DIM], axis=1).reshape(heads, 2)
    bias_part = lax.dynamic_update_slice_in_dim(jnp.zeros((heads * chips, 2), F32), bias_part, chip * heads, 0)
    gain_parts = gain_rows[:2, :HEAD_DIM] + gain_rows[:2, HEAD_DIM:]
    packed = [gain1_part, gain2_part, bias_part[:, 0], bias_part[:, 1], gain_parts[0], gain_parts[1]]
    packed = jnp.concatenate([a.reshape(fsdp, -1) for a in packed], axis=1)
    packed = jnp.pad(packed[:, None], ((0, 0), (0, PAD - 1), (0, 3 * width - packed.shape[1])))
    qkv_sum = core_sum(grad_qkv.reshape(fsdp, 2, half_z, 3 * width))
    qkv_z = z_sum(jnp.concatenate([qkv_sum, packed.astype(BF)], axis=1)).astype(BF)
    qkv_all = all_pieces(qkv_z)
    small_sum = jnp.sum(qkv_all[:, :, half_z].astype(F32), axis=(0, 1))
    small_out = [small_sum[a:b] for a, b in zip(cuts[:-1], cuts[1:])]
    grads = qkv_all[:, :, :half_z].reshape(chips, rows_z, 3, width).transpose(2, 1, 0, 3)
    grads = grads.reshape(3, rows_z, model).astype(F32)
    return (
        output, grad_inputs, grads[0], grads[1], grads[2], total_o, total_gu[0], total_gu[1], total_d,
        small_out[0], small_out[1], jnp.stack([small_out[2], small_out[3]], axis=1), small_out[4], small_out[5],
    )


def solution(mesh):
    rows, row = P("fsdp", None), P("fsdp")
    block, ids = P("fsdp", "ctx", None), P("fsdp", "ctx")
    return jax.shard_map(
        functools.partial(layer, mesh.shape["ctx"], mesh.shape["fsdp"]),
        mesh=mesh,
        in_specs=(block, ids, ids, row) + (rows,) * 7 + (row, row, rows, row, row, block),
        out_specs=(block, block) + (rows,) * 7 + (row, row, rows, row, row),
        check_vma=False,
    )
```

```python
import functools

import jax
import jax.numpy as jnp
import ml_dtypes
import numpy as np
from jax import lax
from jax.experimental import pallas as pl
from jax.experimental.pallas import tpu as pltpu
from jax.sharding import Mesh
from jax.sharding import PartitionSpec as P

EPSILON = 1e-05
ROPE_BASE = 10000.0
NEG_FILL = -1e30
HEAD_DIM = 64
HALF = HEAD_DIM // 2
BF = jnp.bfloat16
F32 = jnp.float32
PAD = 16
LANES = 128
PEAK = 3.45e9

NT = (((1,), (1,)), ((), ()))
TN = (((0,), (0,)), ((), ()))
NN = (((1,), (0,)), ((), ()))

Q_ROW, K_ROW, SAME_ROW, OTHER_ROW = 4, 5, 6, 7


def mm(left, right, dims=NN):
    return lax.dot_general(left, right, dims, preferred_element_type=F32)


class Far:
    def __init__(self, array):
        self.array = array


def kernel_call(kernel, out_shapes, *operands, scalars=None, scratch=(), us=1.0, vmem=24, after=()):
    far_in = [isinstance(a, Far) for a in operands]
    far_out = [isinstance(a, Far) for a in out_shapes]
    operands = [a.array if isinstance(a, Far) else a for a in operands]
    out_shapes = [a.array if isinstance(a, Far) else a for a in out_shapes]
    n_in, n_out, n_own = len(operands), len(out_shapes), len(scratch)
    vmem_spec, any_spec = pl.BlockSpec(memory_space=pltpu.VMEM), pl.BlockSpec(memory_space=pl.ANY)
    specs = [any_spec if far else vmem_spec for far in far_in] + [any_spec] * len(after)
    first = 0
    all_operands = list(operands) + list(after)
    if scalars is not None:
        specs = [pl.BlockSpec(memory_space=pltpu.SMEM)] + specs
        all_operands = [scalars] + all_operands
        first = 1
    fetched = [pltpu.VMEM(a.shape, a.dtype) for a, far in zip(operands, far_in) if far]
    shipped = [pltpu.VMEM(a.shape, a.dtype) for a, far in zip(out_shapes, far_out) if far]
    n_sems = len(fetched) + len(shipped)
    sems = [pltpu.SemaphoreType.DMA((n_sems,))] if n_sems else []

    def whole(*refs):
        head, refs = list(refs[:first]), refs[first:]
        ins, refs = list(refs[:n_in]), refs[n_in + len(after) :]
        outs, refs = list(refs[:n_out]), refs[n_out:]
        own, refs = list(refs[:n_own]), refs[n_own:]
        local, sem, copies = 0, refs[-1] if n_sems else None, []
        for n in range(n_in):
            if far_in[n]:
                copies.append(pltpu.make_async_copy(ins[n], refs[local], sem.at[local]))
                copies[-1].start()
                ins[n] = refs[local]
                local += 1
        ship, waits = [], []
        for n in range(n_out):
            if far_out[n]:

                def start(source=refs[local], target=outs[n], at=local, started=[]):
                    if not started:
                        started.append(pltpu.make_async_copy(source, target, sem.at[at]))
                        started[0].start()
                        waits.append(started[0])

                ship.append(start)
                outs[n] = refs[local]
                local += 1
        for copy in copies:
            copy.wait()
        extra = {"ship": ship} if ship else {}
        kernel(*head, *ins, *outs, *own, **extra)
        for start in ship:
            start()
        for copy in waits:
            copy.wait()

    return pl.pallas_call(
        whole,
        out_shape=out_shapes,
        in_specs=specs,
        out_specs=[any_spec if far else vmem_spec for far in far_out],
        scratch_shapes=list(scratch) + fetched + shipped + sems,
        cost_estimate=pl.CostEstimate(flops=int(us * PEAK), bytes_accessed=0, transcendentals=0),
        compiler_params=pltpu.CompilerParams(vmem_limit_bytes=vmem * 2**20),
    )(*all_operands)


def shape_of(dims, dtype):
    return jax.ShapeDtypeStruct(tuple(dims), dtype)


def stack_rows(*parts, after=()):
    def kernel(*refs):
        at = 0
        for ref in refs[:-1]:
            refs[-1][pl.ds(at, ref.shape[0]), :] = ref[...]
            at += ref.shape[0]

    rows = sum(a.shape[0] for a in parts)
    out = shape_of((rows, parts[0].shape[1]), parts[0].dtype)
    return kernel_call(kernel, [out], *[Far(a) for a in parts], after=after)[0]


def pair_kernel(where, both, own, other):
    own[...] = both[where[0]]
    other[...] = both[1 - where[0]]


def lane_of(shape):
    return lax.broadcasted_iota(jnp.int32, shape, 1)


def head_sum(values):
    row = lax.broadcasted_iota(jnp.int32, (LANES, LANES), 0) // HEAD_DIM
    col = lax.broadcasted_iota(jnp.int32, (LANES, LANES), 1) // HEAD_DIM
    ones = (row == col).astype(BF)
    high = values.astype(BF)
    low = (values - high.astype(F32)).astype(BF)
    return mm(high, ones) + mm(low, ones)


def half_swap(values):
    first = lane_of(values.shape) % HEAD_DIM < HALF
    return jnp.where(first, pltpu.roll(values, LANES - HALF, 1), pltpu.roll(values, HALF, 1))


def rotary(table):
    lane = lane_of(table.shape)
    base = jnp.where(lane < HEAD_DIM, table, pltpu.roll(table, HEAD_DIM, 1))
    other = half_swap(base)
    first = lane % HEAD_DIM < HALF
    return jnp.where(first, base, other), jnp.where(first, -other, base)


def one_lane(row, index):
    return jnp.sum(jnp.where(lane_of(row.shape) == index, row, 0.0), axis=1, keepdims=True)


def key_features(kind, params, head):
    same = one_lane(params[SAME_ROW : SAME_ROW + 1, :LANES], head)
    other = one_lane(params[OTHER_ROW : OTHER_ROW + 1, :LANES], head)
    return jnp.where(kind == 0.0, other, jnp.where(kind == 1.0, same, NEG_FILL)).astype(BF)


def load_halves(refs, places):
    return [refs[n][pl.ds(at, count), :] for n, at, count in places]


def scale_of(x):
    return lax.rsqrt(jnp.mean(x * x, axis=-1, keepdims=True) + EPSILON)


def norm_back(grad, x, gain):
    scale = scale_of(x)
    unit = x * scale
    scaled = grad * gain
    return scale * (scaled - unit * jnp.mean(scaled * unit, axis=-1, keepdims=True))


def input_kernel(where, inputs, times, variates, own, other):
    slots = inputs.shape[1]
    for index, out in ((where[0], own), (1 - where[0], other)):
        out[pl.ds(0, slots), :] = inputs[index]
        time, variate = times[pl.ds(index, 1), :], variates[pl.ds(index, 1), :]
        rows = [time >> 8, time & 255, variate, jnp.zeros((PAD - 3, slots), jnp.int32)]
        out[pl.ds(slots, PAD), :] = jnp.zeros((PAD, out.shape[1]), BF)
        out[pl.ds(slots, PAD), pl.ds(0, slots)] = jnp.concatenate(rows, 0).astype(F32).astype(BF)


def weight_kernel(width, where, w_query, w_key, w_value, gain_attn, gain_ffn, head_bias, q_gain, k_gain, out):
    core, chip, depth = where[0], where[1], where[2]
    half = w_query.shape[0] // 2
    blocks = width // LANES
    at = 0
    for ref in (w_query, w_key, w_value):
        for n in range(blocks):
            col = pl.multiple_of(chip * width + n * LANES, LANES)
            row = pl.multiple_of(core * half, 16)
            out[pl.ds(at, half), :] = ref[pl.ds(row, half), pl.ds(col, LANES)]
            at += half
    lane = lane_of((1, LANES))
    rows = [gain_attn[...].astype(F32), gain_ffn[...].astype(F32)]
    rows = [jnp.concatenate([r, jnp.zeros((2 - r.shape[0], LANES), F32)], 0) if r.shape[0] < 2 else r for r in rows]
    for ref in (q_gain, k_gain):
        value, dims = ref[...].astype(F32), ref.shape[1]
        row = jnp.zeros((1, LANES), F32)
        for j in range(dims):
            row = jnp.where(lane % HEAD_DIM == depth * dims + j, value[:, j : j + 1], row)
        rows.append(row)
    value, heads = head_bias[...].astype(F32), head_bias.shape[0]
    for n in range(2):
        row = jnp.zeros((1, LANES), F32)
        for j in range(heads):
            row = jnp.where(lane == depth * heads + j, value[j : j + 1, n : n + 1], row)
        rows.append(row)
    rows.append(jnp.zeros((PAD - 8, LANES), F32))
    out[pl.ds(at, PAD), :] = jnp.concatenate(rows, 0).astype(BF)


def turn_table(span):
    coarse = -(-span // 16)
    frequency = ROPE_BASE ** (-np.arange(HALF) * (2.0 / HEAD_DIM))
    steps = np.concatenate([16.0 * np.arange(coarse), np.arange(16.0)])
    angles = steps[:, None] * frequency
    exact = np.concatenate([np.cos(angles), np.sin(angles)], axis=1).astype(np.float32)
    parts, rest = [], exact
    for _ in range(3):
        low = rest.astype(ml_dtypes.bfloat16)
        parts.append(low)
        rest = rest - low.astype(np.float32)
    return np.concatenate(parts, axis=1)


def slot_table(where, ids, turns, slots, d):
    tables = []
    coarse = turns.shape[0] - 16
    for c in range(2):
        rows = ids[c][:, :slots].astype(F32)
        high, low, variate = rows[0:1].astype(jnp.int32), rows[1:2].astype(jnp.int32), rows[2:3].astype(jnp.int32)
        time = high * 256 + low
        index = lax.broadcasted_iota(jnp.int32, (coarse, slots), 0)
        hot_a = jnp.where(index == time >> 4, 1.0, 0.0).astype(BF)
        index = lax.broadcasted_iota(jnp.int32, (16, slots), 0)
        hot_b = jnp.where(index == (time & 15), 1.0, 0.0).astype(BF)
        turn_a, turn_b = mm(hot_a, turns[:coarse], TN), mm(hot_b, turns[coarse:], TN)
        turn_a = turn_a[:, :64] + turn_a[:, 64:128] + turn_a[:, 128:]
        turn_b = turn_b[:, :64] + turn_b[:, 64:128] + turn_b[:, 128:]
        cos_a, sin_a, cos_b, sin_b = turn_a[:, :HALF], turn_a[:, HALF:], turn_b[:, :HALF], turn_b[:, HALF:]
        index = lax.broadcasted_iota(jnp.int32, (HEAD_DIM, slots), 0)
        hot = jnp.where(index == variate, 1.0, 0.0).astype(BF)
        eye = lax.broadcasted_iota(jnp.int32, (HEAD_DIM, HEAD_DIM), 0) == lane_of((HEAD_DIM, HEAD_DIM))
        kind = mm(hot, jnp.where(eye, 1.0, 0.0).astype(BF), TN)
        tables.append(jnp.concatenate([cos_a * cos_b - sin_a * sin_b, sin_a * cos_b + cos_a * sin_b, kind], axis=1))
    table = jnp.concatenate(tables, axis=0)
    hidden = jnp.logical_and(lane_of(table.shape) >= HEAD_DIM, jnp.logical_not(valid_rows(where, 2, slots, d)))
    return jnp.where(hidden, 2.0, table)


def front_kernel(cfg, where, *refs, ship):
    chips, width, heads, depths, places = cfg
    n_x = 1 + max(n for pair in places for n, _, _ in pair)
    xs, refs = refs[:n_x], refs[n_x:]
    turns, packed, q, k, v, pre, n1, w, mix, tables, params = refs[:11]
    lows, kinds, hots = refs[11 : 11 + chips], refs[11 + chips], refs[12 + chips]
    chunk = q.shape[0] // chips
    slots = chunk // 2
    model = n1.shape[1]
    half = model // depths // 2
    blocks = 3 * width // LANES
    piece = blocks * half + PAD
    for z in range(depths):
        for c in range(2):
            base = (2 * z + c) * piece
            for n in range(blocks):
                w[pl.ds((2 * z + c) * half, half), pl.ds(n * LANES, LANES)] = packed[pl.ds(base + n * half, half), :]
    ship[5]()
    smalls = [packed[pl.ds(2 * z * piece + blocks * half, PAD), :].astype(F32) for z in range(depths)]
    per = 2 * half // LANES
    gain1 = jnp.concatenate([a[n : n + 1] for a in smalls for n in range(max(per, 1))], 1)
    gain2 = jnp.concatenate([a[2 + n : 3 + n] for a in smalls for n in range(max(per, 1))], 1)
    total = functools.reduce(lambda a, b: a + b, smalls)
    params[...] = jnp.zeros_like(params)
    params[pl.ds(0, 1), :] = gain1
    params[pl.ds(1, 1), :] = gain2
    for n in (Q_ROW, K_ROW, SAME_ROW, OTHER_ROW):
        params[pl.ds(n, 1), pl.ds(0, LANES)] = total[n : n + 1]
    for d in range(chips):
        rows = pl.ds(d * chunk, chunk)
        ids = [xs[n][pl.ds(at + slots, PAD), :] for n, at, _ in places[d]]
        table = slot_table(where, ids, turns[...], slots, d)
        tables[rows, :] = table
        cosine, sine = rotary(table)
        kind = table[:, HEAD_DIM:]
        kinds[rows, :] = kind.astype(BF)
        hots[rows, :] = (kind == 1.0).astype(BF)
        x = jnp.concatenate(load_halves(xs, places[d]), axis=0).astype(F32)
        low = (x * scale_of(x) * gain1).astype(BF)
        n1[rows, :] = low
        both = mm(low, w[...])
        v[rows, :] = both[:, 2 * width :].astype(BF)
        pre[rows, :] = both[:, : 2 * width]
        for source, row, target in ((0, Q_ROW, q), (width, K_ROW, k)):
            gain = total[row : row + 1]
            for g in range(width // LANES):
                value = both[:, source + LANES * g : source + LANES * (g + 1)]
                scale = lax.rsqrt(head_sum(value * value) * (1.0 / HEAD_DIM) + EPSILON)
                normed = value * scale * gain
                target[rows, pl.ds(LANES * g, LANES)] = (normed * cosine + half_swap(normed) * sine).astype(BF)
    for n in (0, 1, 2, 3, 4, 7):
        ship[n]()
    for h in range(heads):
        lanes = pl.ds(HEAD_DIM * h, HEAD_DIM)
        features = key_features(kinds[...].astype(F32), total, where[1] * heads + h)
        keys = jnp.concatenate([k[:, lanes], features], axis=1)
        values = v[:, lanes]
        for d in range(chips):
            rows = pl.ds(d * chunk, chunk)
            query = jnp.concatenate([q[rows, lanes] * BF(0.125), hots[rows, :]], axis=1)
            terms = jnp.exp(mm(query, keys, NT))
            denom = jnp.sum(terms, axis=-1, keepdims=True)
            part = mm(terms.astype(BF), values) / denom
            mix[rows, lanes] = part
            lows[d][:, lanes] = part.astype(BF)


def mix_out_kernel(width, chips, where, own, w_out, params, *refs):
    pieces, (h_ref, n2) = refs[:chips], refs[chips:]
    chunk = h_ref.shape[0]
    slots = chunk // 2
    total = None
    for d in range(chips):
        row = pl.multiple_of((where[1] ^ d) * width, LANES)
        term = mm(pieces[d][...], w_out[pl.ds(row, width), :])
        total = term if total is None else total + term
    x = jnp.concatenate([own[pl.ds(0, slots), :], own[pl.ds(slots + PAD, slots), :]], axis=0)
    h = x.astype(F32) + total
    h_ref[...] = h
    n2[...] = (h * scale_of(h) * params[pl.ds(1, 1), :]).astype(BF)


def valid_rows(where, halves, slots, d):
    row = lax.broadcasted_iota(jnp.int32, (slots, 1), 0)
    here = where[5]
    return jnp.concatenate([(here ^ (2 * d + c)) * slots + row < where[6 + where[0]] for c in range(halves)], axis=0)


def pack_kernel(cfg, where, w_gate, w_up, w_down, packed):
    chips, depths, ff, ff_z = cfg
    half, hidden = w_gate.shape[0] // 2, w_gate.shape[1]
    model = w_down.shape[1]
    blocks = -(-2 * ff // LANES)
    padded = -(-ff_z // 16) * 16
    quarters = model // 2 // LANES
    core = where[0]
    rows = pl.ds(pl.multiple_of(core * half, 16), half)
    for t in range(chips):

        @pl.when(where[1] == t)
        def _():
            parts = []
            for ref in (w_gate, w_up):
                both = ref[rows, :]
                parts += [both[:, n * (hidden // depths) + t * ff_z :][:, :ff_z] for n in range(depths)]
            if 2 * ff % LANES:
                parts.append(jnp.zeros((half, blocks * LANES - 2 * ff), BF))
            tight = jnp.concatenate(parts, axis=1)
            for n in range(blocks):
                packed[pl.ds(n * half, half), :] = tight[:, n * LANES : (n + 1) * LANES]
            for n in range(quarters):
                col = pl.multiple_of(core * (model // 2) + n * LANES, LANES)
                value = w_down[pl.ds(t * ff_z, ff_z), pl.ds(col, LANES)]
                if padded > ff_z:
                    value = jnp.concatenate([value, jnp.zeros((padded - ff_z, LANES), BF)], axis=0)
                packed[pl.ds(blocks * half + n * padded, padded), :] = value


def unpack_kernel(cfg, packed, w_gu, w_d):
    depths, ff, ff_z, ff_pad = cfg
    model = w_gu.shape[0]
    half = model // depths // 2
    blocks = -(-2 * ff // LANES)
    padded = -(-ff_z // 16) * 16
    quarters = model // 2 // LANES
    piece = blocks * half + quarters * padded
    w_gu[...] = jnp.zeros_like(w_gu)
    w_d[...] = jnp.zeros_like(w_d)
    for z in range(depths):
        for c in range(2):
            base = (2 * z + c) * piece
            rows = pl.ds((2 * z + c) * half, half)
            both = jnp.concatenate([packed[pl.ds(base + n * half, half), :] for n in range(blocks)], axis=1)
            w_gu[rows, pl.ds(0, ff)] = both[:, :ff]
            w_gu[rows, pl.ds(ff_pad, ff)] = both[:, ff : 2 * ff]
            for n in range(quarters):
                at = base + blocks * half + n * padded
                w_d[pl.ds(z * ff_z, ff_z), pl.ds(c * model // 2 + n * LANES, LANES)] = packed[pl.ds(at, ff_z), :]


def ffn_kernel(cfg, where, *refs):
    d, n2_places, dy_places, ff_pad = cfg
    n_n2 = 1 + max(n for n, _, _ in n2_places)
    n_dy = 1 + max(n for n, _, _ in dy_places)
    n2s, dys, refs = refs[:n_n2], refs[n_n2 : n_n2 + n_dy], refs[n_n2 + n_dy :]
    w_gu, w_d, dn2, act, dgu = refs
    n2 = jnp.concatenate(load_halves(n2s, n2_places), axis=0)
    dy = jnp.concatenate(load_halves(dys, dy_places), axis=0)
    dy = jnp.where(valid_rows(where, 2, n2.shape[0] // 2, d), dy, jnp.zeros_like(dy))
    pre = mm(n2, w_gu[...])
    gate, up = pre[:, :ff_pad], pre[:, ff_pad:]
    sig = jax.nn.sigmoid(gate)
    silu = gate * sig
    low = (silu * up).astype(BF)
    act[...] = low
    d_act = mm(dy, w_d[...], NT)
    d_up = (d_act * silu).astype(BF)
    d_gate = (d_act * up * sig * (1.0 + gate * (1.0 - sig))).astype(BF)
    both = jnp.concatenate([d_gate, d_up], axis=1)
    dgu[...] = both
    dn2[...] = mm(both, w_gu[...], NT).astype(BF)


def down_kernel(chips, *refs):
    acts, w_d, outs = refs[:chips], refs[chips], refs[chips + 1 :]
    for act, out in zip(acts, outs):
        out[...] = mm(act[...], w_d[...]).astype(BF)


def ffn_grad_kernel(cfg, where, *refs):
    chips, depths, ff, ff_z, ff_pad, n2_places, dy_places = cfg
    n_n2 = 1 + max(n for pair in n2_places for n, _, _ in pair)
    n_dy = 1 + max(n for pair in dy_places for n, _, _ in pair)
    n2s, dys, refs = refs[:n_n2], refs[n_n2 : n_n2 + n_dy], refs[n_n2 + n_dy :]
    acts, dgus, (w_gu, params, packed, gain2, n2, dy, act, dgu) = refs[:chips], refs[chips : 2 * chips], refs[2 * chips :]
    model = w_gu.shape[0]
    chunk = acts[0].shape[0]
    for d in range(chips):
        rows = pl.ds(d * chunk, chunk)
        n2[rows, :] = jnp.concatenate(load_halves(n2s, n2_places[d]), axis=0)
        part = jnp.concatenate(load_halves(dys, dy_places[d]), axis=0)
        dy[rows, :] = jnp.where(valid_rows(where, 2, chunk // 2, d), part, jnp.zeros_like(part))
        act[rows, :] = acts[d][...]
        dgu[rows, :] = dgus[d][...]
    half = model // depths // 2
    blocks = -(-2 * ff // LANES)
    padded = -(-ff_z // 16) * 16
    quarters = model // 2 // LANES
    piece = blocks * half + quarters * padded
    for b in range(2 * depths):
        rows = pl.ds(b * half, half)
        grad = mm(n2[:, rows], dgu[...], TN)
        gain2[rows, :] = jnp.sum(grad * w_gu[rows, :].astype(F32), axis=1, keepdims=True)
        tight = jnp.concatenate([grad[:, :ff], grad[:, ff_pad : ff_pad + ff]], axis=1).astype(BF)
        if 2 * ff % LANES:
            tight = jnp.concatenate([tight, jnp.zeros((half, blocks * LANES - 2 * ff), BF)], axis=1)
        for n in range(blocks):
            packed[pl.ds(b * piece + n * half, half), :] = tight[:, n * LANES : (n + 1) * LANES]
    for z in range(depths):
        grad = mm(act[:, pl.ds(z * ff_z, ff_z)], dy[...], TN).astype(BF)
        if padded > ff_z:
            grad = jnp.concatenate([grad, jnp.zeros((padded - ff_z, model), BF)], axis=0)
        for c in range(2):
            for n in range(quarters):
                at = (2 * z + c) * piece + blocks * half + n * padded
                col = c * model // 2 + n * LANES
                packed[pl.ds(at, padded), :] = grad[:, col : col + LANES]


def ffn_final_kernel(cfg, packed, g_gate, g_up, g_down):
    chips, depths, ff, ff_z = cfg
    model = g_down.shape[1]
    half = model // depths // 2
    hidden_z = chips * ff_z
    blocks = -(-2 * ff // LANES)
    padded = -(-ff_z // 16) * 16
    quarters = model // 2 // LANES
    piece = blocks * half + quarters * padded
    for t in range(chips):
        for c in range(2):
            base = (2 * t + c) * piece
            both = jnp.concatenate([packed[pl.ds(base + n * half, half), :] for n in range(blocks)], axis=1).astype(F32)
            for z in range(depths):
                cols = pl.ds(z * hidden_z + t * ff_z, ff_z)
                g_gate[pl.ds(c * half, half), cols] = both[:, z * ff_z : (z + 1) * ff_z]
                g_up[pl.ds(c * half, half), cols] = both[:, ff + z * ff_z : ff + (z + 1) * ff_z]
            for n in range(quarters):
                at = base + blocks * half + n * padded
                rows = pl.ds(t * ff_z, ff_z)
                g_down[rows, pl.ds(c * model // 2 + n * LANES, LANES)] = packed[pl.ds(at, ff_z), :].astype(F32)


def output_kernel(chips, where, h, *refs):
    terms, (out, low) = refs[:chips], refs[chips:]
    slots = out.shape[0]
    total = h[...]
    for ref in terms:
        total = total + ref[...].astype(F32)
    total = jnp.where(valid_rows(where, 2, slots, 0), total, 0.0).astype(BF)
    out[...] = total[:slots]
    low[...] = total[slots:]


def hidden_back_kernel(width, chips, where, h, dy, params, w_out, *refs):
    terms, (d_h, d_low), d_mix = refs[:chips], refs[chips : chips + 2], refs[chips + 2 :]
    grad = terms[0][...].astype(F32)
    for ref in terms[1:]:
        grad = grad + ref[...].astype(F32)
    own = jnp.where(valid_rows(where, 2, dy.shape[0] // 2, 0), dy[...].astype(F32), 0.0)
    total = own + norm_back(grad, h[...], params[pl.ds(1, 1), :])
    d_h[...] = total
    low = total.astype(BF)
    d_low[...] = low
    for d in range(chips):
        row = pl.multiple_of((where[1] ^ d) * width, LANES)
        d_mix[d][...] = mm(low, w_out[pl.ds(row, width), :], NT).astype(BF)


def out_grad_kernel(cfg, where, d_low, *refs):
    chips, depths, width, piece = cfg
    mixes, (mine, theirs, full) = refs[:chips], refs[chips:]
    core, chip, depth = where[0], where[1], where[2]
    rows_z = full.shape[0] // depths
    for d in range(chips):
        row = pl.multiple_of((chip ^ d) * width, LANES)
        full[pl.ds(row, width), :] = mm(mixes[d][...], d_low[...], TN)
    for out, c in ((mine, core), (theirs, 1 - core)):
        for d in range(chips):
            for p in range(depths):
                row = (depth ^ p) * rows_z + c * (rows_z // 2) + (chip ^ d) * piece
                out[d, p] = full[pl.ds(pl.multiple_of(row, 8), piece), :].astype(BF)


def sum_kernel(split, *refs):
    outs, terms = refs[len(refs) - split :], refs[: len(refs) - split]
    for n, out in enumerate(outs):
        pick = (lambda ref: ref[n]) if split > 1 else (lambda ref: ref[...])
        total = pick(terms[0]).astype(F32)
        for ref in terms[1:]:
            total = total + pick(ref).astype(F32)
        out[...] = total.astype(out.dtype)


def summed(terms, split):
    dims = terms[0].shape[1:] if split > 1 else terms[0].shape
    return kernel_call(functools.partial(sum_kernel, split), [shape_of(dims, BF)] * split, *terms)


def input_back_kernel(chips, own_x, d_h, params, *refs):
    terms, (out, low) = refs[:chips], refs[chips:]
    slots = out.shape[0]
    grad = terms[0][...].astype(F32)
    for ref in terms[1:]:
        grad = grad + ref[...].astype(F32)
    x = jnp.concatenate([own_x[pl.ds(0, slots), :], own_x[pl.ds(slots + PAD, slots), :]], axis=0).astype(F32)
    total = d_h[...] + norm_back(grad, x, params[pl.ds(0, 1), :])
    out[...] = total[:slots]
    low[...] = total[slots:].astype(BF)


def attend_back_kernel(cfg, where, *refs):
    chips, heads, width = cfg
    dmixes, refs = refs[:chips], refs[chips:]
    tables, q, k, v, mix, pre, params, d_qkv, smalls = refs[:9]
    dmix, kinds, hots, dq_scr, dk_scr, dv_scr = refs[9:]
    span = k.shape[0]
    chunk = span // chips
    dk_scr[...] = jnp.zeros_like(dk_scr)
    dv_scr[...] = jnp.zeros_like(dv_scr)
    smalls[...] = jnp.zeros_like(smalls)
    for d in range(chips):
        rows = pl.ds(d * chunk, chunk)
        dmix[rows, :] = dmixes[d][...]
        kind = tables[rows, HEAD_DIM:]
        kinds[rows, :] = kind.astype(BF)
        hots[rows, :] = (kind == 1.0).astype(BF)
    lane = lane_of((1, LANES))

    def step(c, carry):
        part = pl.ds(pl.multiple_of(c * chunk, chunk), chunk)
        query_hot = hots[part, :]
        for h in range(heads):
            lanes = pl.ds(HEAD_DIM * h, HEAD_DIM)
            key = k[:, lanes]
            index = where[1] * heads + h
            keys = jnp.concatenate([key, key_features(kinds[...].astype(F32), params, index)], axis=1)
            query = q[part, lanes] * BF(0.125)
            grad = dmix[part, lanes]
            product = mix[part, lanes] * grad.astype(F32)
            high = product.astype(BF)
            low = (product - high.astype(F32)).astype(BF)
            ones = jnp.ones((8, HEAD_DIM), BF)
            delta = (mm(ones, high, NT) + mm(ones, low, NT))[:1]
            terms = jnp.exp(mm(keys, jnp.concatenate([query, query_hot], axis=1), NT))
            prob = terms * (1.0 / jnp.sum(terms, axis=0, keepdims=True))
            d_score = (prob * (mm(v[:, lanes], grad, NT) - delta)).astype(BF)
            dk_scr[:, lanes] += mm(d_score, query)
            dv_scr[:, lanes] += mm(prob.astype(BF), grad)
            both = mm(d_score, jnp.concatenate([key, hots[...]], axis=1), TN)
            dq_scr[part, lanes] = both[:, :HEAD_DIM] * 0.125
            pairs = both[:, HEAD_DIM:]
            hot = query_hot.astype(F32)
            for row, weight in ((SAME_ROW, hot), (OTHER_ROW, 1.0 - hot)):
                value = jnp.sum(jnp.sum(pairs * weight, axis=0, keepdims=True), axis=1, keepdims=True)
                smalls[pl.ds(row, 1), :] += jnp.where(lane == index, value, 0.0)
        return carry

    lax.fori_loop(0, chips, step, 0)
    for d in range(chips):
        part = pl.ds(d * chunk, chunk)
        cosine, sine = rotary(tables[part, :])
        for n, (grads, row) in enumerate(((dq_scr, Q_ROW), (dk_scr, K_ROW))):
            gain = params[pl.ds(row, 1), pl.ds(0, LANES)]
            for g in range(width // LANES):
                grad = grads[part, pl.ds(LANES * g, LANES)]
                value = pre[part, pl.ds(n * width + LANES * g, LANES)]
                scale = lax.rsqrt(head_sum(value * value) * (1.0 / HEAD_DIM) + EPSILON)
                unit = value * scale
                d_normed = grad * cosine - half_swap(grad) * sine
                total = jnp.sum(d_normed * unit, axis=0, keepdims=True)
                smalls[pl.ds(row, 1), :] += total + pltpu.roll(total, HEAD_DIM, 1)
                scaled = d_normed * gain
                mean = head_sum(scaled * unit) * (1.0 / HEAD_DIM)
                d_qkv[part, pl.ds(n * width + LANES * g, LANES)] = (scale * (scaled - unit * mean)).astype(BF)
        d_qkv[part, pl.ds(2 * width, width)] = dv_scr[part, :].astype(BF)


def qkv_grad_kernel(depths, where, n1, d_qkv, w, mine, theirs, gain1, full):
    core, depth = where[0], where[2]
    model = n1.shape[1]
    half = model // depths // 2
    tile = 256
    for n in range(model // tile):
        rows = pl.ds(n * tile, tile)
        grad = mm(n1[:, rows], d_qkv[...], TN)
        full[rows, :] = grad
        gain1[rows, :] = jnp.sum(grad * w[rows, :].astype(F32), axis=1, keepdims=True)
    for out, c in ((mine, core), (theirs, 1 - core)):
        for p in range(depths):
            row = pl.multiple_of((2 * (depth ^ p) + c) * half, 16)
            out[pl.ds(p * half, half), :] = full[pl.ds(row, half), :].astype(BF)


def project_back_kernel(d_qkv, w, *outs):
    chunk = outs[0].shape[0]
    for n, out in enumerate(outs):
        out[...] = mm(d_qkv[pl.ds(n * chunk, chunk), :], w[...], NT).astype(BF)


def qkv_message_kernel(depths, where, mine, got, smalls, *outs):
    half = mine.shape[0] // depths
    for p, out in enumerate(outs):
        rows = pl.ds(p * half, half)
        out[pl.ds(0, half), :] = (mine[rows, :].astype(F32) + got[rows, :].astype(F32)).astype(BF)
        out[pl.ds(half, PAD), :] = jnp.zeros((PAD, out.shape[1]), BF)
        out[pl.ds(half, PAD), pl.ds(0, LANES)] = smalls[where[2] ^ p].astype(BF)


def qkv_final_kernel(cfg, where, *refs):
    chips, width, places, half = cfg
    n_same = 1 + max(n for pair in places for n, _, _ in pair)
    same, (other, g_q, g_k, g_v, smalls) = refs[:n_same], refs[n_same:]
    core, chip = where[0], where[1]
    piece = half + PAD
    total = None
    for c in range(2):
        row = pl.multiple_of((core if c == 0 else 1 - core) * half, 16)
        for d in range(chips):
            if c == 0:
                parts = load_halves(same, places[d])
                value = jnp.concatenate(parts, axis=0) if len(parts) > 1 else parts[0]
            else:
                value = other[pl.ds(d * piece, piece), :]
            col = pl.multiple_of((chip ^ d) * width, LANES)
            value = value.astype(F32)
            for n, out in enumerate((g_q, g_k, g_v)):
                out[pl.ds(row, half), pl.ds(col, width)] = value[:half, n * width : (n + 1) * width]
            small = value[half:, :LANES]
            total = small if total is None else total + small
    smalls[...] = total


def out_final_kernel(cfg, where, *refs):
    chips, places, piece, half = cfg
    n_same = 1 + max(n for pair in places for n, _, _ in pair)
    same, (other, out) = refs[:n_same], refs[n_same:]
    core, chip = where[0], where[1]
    for c in range(2):
        for d in range(chips):
            if c == 0:
                parts = load_halves(same, places[d])
                value = jnp.concatenate(parts, axis=0) if len(parts) > 1 else parts[0]
            else:
                value = other[pl.ds(d * piece, piece), :]
            row = (core if c == 0 else 1 - core) * half + (chip ^ d) * piece
            out[pl.ds(pl.multiple_of(row, 8), piece), :] = value.astype(F32)


def w_out_kernel(cfg, where, *refs):
    chips, depths, places, piece = cfg
    n_same = 1 + max(n for pair in places for n, _, _ in pair)
    same, (other, out, full) = refs[:n_same], refs[n_same:]
    here, depth = where[5], where[2]
    rows_z = out.shape[0] // depths
    for c in range(2):
        for d in range(chips):
            if c == 0:
                parts = load_halves(same, places[d])
                value = jnp.concatenate(parts, axis=0) if len(parts) > 1 else parts[0]
            else:
                value = other[pl.ds(d * depths * piece, depths * piece), :]
            value = value.astype(F32)
            for p in range(depths):
                row = (depth ^ p) * rows_z + (here ^ (2 * d + c)) * piece
                full[pl.ds(pl.multiple_of(row, 8), piece), :] = value[p * piece : (p + 1) * piece]
    out[...] = full[...].astype(BF)


def layer(
    chips, fsdp, inputs, time_ids, variate_ids, seq_lengths, w_query, w_key, w_value, w_out, w_gate,
    w_up, w_down, gain_attn, gain_ffn, head_bias, q_gain, k_gain, cotangent,
):
    _, slots, model = inputs.shape
    heads = model // HEAD_DIM // chips
    width = heads * HEAD_DIM
    rows_z = w_query.shape[0]
    half_z = rows_z // 2
    hidden = w_gate.shape[1]
    ff = hidden // chips
    ff_z = ff // fsdp
    ff_pad = -(-ff // 256) * 256
    chunk = 2 * slots
    span = chips * chunk
    core, chip, depth = lax.axis_index("core"), lax.axis_index("chip"), lax.axis_index("fsdp")
    here = 2 * chip + core
    heads_z, dims_z = head_bias.shape[0], q_gain.shape[0]
    place = jnp.stack([core, chip, depth, heads_z, dims_z, here]).astype(jnp.int32)
    where = jnp.concatenate([place, seq_lengths])

    def pc(a):
        return lax.ppermute(a, "core", [(0, 1), (1, 0)])

    def pt(a, p):
        return lax.ppermute(a, "chip", [(n, n ^ p) for n in range(chips)])

    def pz(a, p):
        return lax.ppermute(a, "fsdp", [(n, n ^ p) for n in range(fsdp)])

    def gather_chips(own):
        rows = own.shape[0]
        if chips == 4:
            cut = rows // 2
            side, up = pt(own, 1), pt(own, 2)
            corner = [pt(side[:cut], 2), pt(up[cut:], 1)]
            places = [[(n, 0, cut), (n, cut, cut)] for n in range(3)] + [[(3, 0, cut), (4, 0, cut)]]
            return [own, side, up] + corner, places
        cut = rows // 2
        got = [own] + [pt(own, d) for d in range(1, chips)]
        return got, [[(n, 0, cut), (n, cut, cut)] for n in range(chips)]

    def exchange(parts):
        return [parts[0]] + [pt(parts[d], d) for d in range(1, chips)]

    def without_pad(places):
        return [[(n, at, count - PAD) for n, at, count in pair] for pair in places]

    x_own, x_other = kernel_call(
        input_kernel, [shape_of((slots + PAD, model), BF)] * 2, inputs, time_ids, variate_ids, scalars=where
    )
    x_chunk = stack_rows(x_own, pc(x_other))
    xs, x_places = gather_chips(x_chunk)

    blocks = 3 * width // LANES
    own_qkv = kernel_call(
        functools.partial(weight_kernel, width),
        [shape_of((blocks * half_z + PAD, LANES), BF)],
        Far(w_query), Far(w_key), Far(w_value), gain_attn.reshape(-1, LANES), gain_ffn.reshape(-1, LANES),
        head_bias, q_gain[None], k_gain[None],
        scalars=where, after=[x_own],
    )[0]
    packed_qkv = lax.all_gather(own_qkv, ("fsdp", "core"), axis=0, tiled=True)

    gu_blocks = -(-2 * ff // LANES)
    quarters = model // 2 // LANES
    padded = -(-ff_z // 16) * 16
    ff_piece = gu_blocks * half_z + quarters * padded
    own_ff = kernel_call(
        functools.partial(pack_kernel, (chips, fsdp, ff, ff_z)), [shape_of((ff_piece, LANES), BF)],
        Far(w_gate), Far(w_up), Far(w_down), scalars=where, after=[x_chunk],
    )[0]
    packed_ff = lax.all_gather(own_ff, ("fsdp", "core"), axis=0, tiled=True)
    w_gu, w_d = kernel_call(
        functools.partial(unpack_kernel, (fsdp, ff, ff_z, ff_pad)),
        [shape_of((model, 2 * ff_pad), BF), shape_of((ff_pad, model), BF)], Far(packed_ff),
    )

    piece = rows_z // (2 * chips)
    own_out = stack_rows(lax.dynamic_slice_in_dim(w_out, here * piece, piece, 0), after=[x_chunk])
    z_out = stack_rows(own_out, *[pz(own_out, p) for p in range(1, fsdp)], after=[xs[1], xs[2]])
    out_same, out_places = gather_chips(z_out)
    out_other = pc(stack_rows(*out_same))
    w_o = kernel_call(
        functools.partial(w_out_kernel, (chips, fsdp, out_places, piece)),
        [shape_of((model, model), BF)], *[Far(a) for a in out_same], Far(out_other),
        scalars=where, scratch=[pltpu.VMEM((model, model), F32)],
    )[0]

    outs = kernel_call(
        functools.partial(front_kernel, (chips, width, heads, fsdp, without_pad(x_places))),
        [Far(shape_of((span, width), BF))] * 3
        + [Far(shape_of((span, 2 * width), F32)), Far(shape_of((span, model), BF))]
        + [Far(shape_of((model, 3 * width), BF)), Far(shape_of((span, width), F32)), Far(shape_of((span, LANES), F32))]
        + [shape_of((8, model), F32)] + [shape_of((chunk, width), BF)] * chips,
        *[Far(a) for a in xs], jnp.asarray(turn_table(span)), Far(packed_qkv),
        scalars=where, us=13.0, vmem=32,
        scratch=[pltpu.VMEM((span, HEAD_DIM), BF)] * 2,
    )
    q, k, v, pre, n1, w_qkv, mix, table, params = outs[:9]

    mix_got = exchange(outs[9:])
    hidden_state, normed2 = kernel_call(
        functools.partial(mix_out_kernel, width, chips),
        [shape_of((chunk, model), F32), shape_of((chunk, model), BF)],
        Far(x_chunk), w_o, params, mix_got[0], *[Far(a) for a in mix_got[1:]],
        scalars=where, us=2.2,
    )

    cot_own, cot_other = kernel_call(
        pair_kernel, [shape_of((slots, model), BF)] * 2, Far(cotangent), scalars=where, after=[z_out]
    )
    dy_chunk = stack_rows(cot_own, pc(cot_other), after=xs[3:])
    dys, dy_places = gather_chips(dy_chunk)
    n2s, n2_places = gather_chips(normed2)

    def refs_of(arrays, pair):
        used = sorted({n for n, _, _ in pair})
        return [arrays[n] for n in used], [(used.index(n), at, count) for n, at, count in pair]

    ffn = []
    for d in range(chips):
        n2_refs, n2_pair = refs_of(n2s, n2_places[d])
        dy_refs, dy_pair = refs_of(dys, dy_places[d])
        ffn.append(
            kernel_call(
                functools.partial(ffn_kernel, (d, n2_pair, dy_pair, ff_pad)),
                [shape_of((chunk, model), BF), shape_of((chunk, ff_pad), BF), shape_of((chunk, 2 * ff_pad), BF)],
                *[Far(a) for a in n2_refs], *[Far(a) for a in dy_refs], w_gu, w_d,
                scalars=where, us=3.3,
            )
        )
    dn2_got = exchange([a[0] for a in ffn])
    outs = kernel_call(
        functools.partial(hidden_back_kernel, width, chips),
        [shape_of((chunk, model), F32), shape_of((chunk, model), BF)] + [shape_of((chunk, width), BF)] * chips,
        hidden_state, Far(dy_chunk), params, w_o, dn2_got[0], *[Far(a) for a in dn2_got[1:]],
        scalars=where, us=2.2,
    )
    d_hidden, d_hidden_low = outs[:2]
    dmix_got = exchange(outs[2:])

    packed_grad, gain2_part = kernel_call(
        functools.partial(ffn_grad_kernel, (chips, fsdp, ff, ff_z, ff_pad, n2_places, dy_places)),
        [shape_of((2 * fsdp * ff_piece, LANES), BF), shape_of((model, 1), F32)],
        *[Far(a) for a in n2s], *[Far(a) for a in dys], *[a[1] for a in ffn], *[a[2] for a in ffn], w_gu, params,
        scalars=where, us=7.6, vmem=36,
        scratch=[pltpu.VMEM((span, n), BF) for n in (model, model, ff_pad, 2 * ff_pad)],
    )
    ff_sum = lax.psum_scatter(packed_grad, ("fsdp", "core"), scatter_dimension=0, tiled=True)
    downs = kernel_call(
        functools.partial(down_kernel, chips), [shape_of((chunk, model), BF)] * chips, *[a[1] for a in ffn], w_d,
        us=1.8, after=[d_hidden_low],
    )
    down_got = exchange(downs)
    own_result, their_result = kernel_call(
        functools.partial(output_kernel, chips), [shape_of((slots, model), BF)] * 2,
        Far(hidden_state), down_got[0], *[Far(a) for a in down_got[1:]], scalars=where,
    )

    def by_sequence(own, other):
        return jnp.where(core == 0, jnp.stack([own, other]), jnp.stack([other, own]))

    output = by_sequence(own_result, pc(their_result))

    mine, theirs = kernel_call(
        functools.partial(out_grad_kernel, (chips, fsdp, width, piece)),
        [shape_of((chips, fsdp, piece, model), BF)] * 2, d_hidden_low, *mix_got,
        scalars=where, us=2.2, scratch=[pltpu.VMEM((model, model), F32)],
    )
    by_chip = summed([mine, pc(theirs)], chips)
    by_depth = summed(exchange(by_chip), fsdp)
    o_piece = summed([by_depth[0]] + [pz(by_depth[p], p) for p in range(1, fsdp)], 1)[0]
    o_same, o_places = gather_chips(o_piece)
    o_other = pc(stack_rows(*o_same))
    grad_out = kernel_call(
        functools.partial(out_final_kernel, (chips, o_places, piece, half_z)),
        [shape_of((rows_z, model), F32)], *o_same, o_other, scalars=where,
    )[0]

    d_qkv, small_part = kernel_call(
        functools.partial(attend_back_kernel, (chips, heads, width)),
        [shape_of((span, 3 * width), BF), shape_of((8, LANES), F32)],
        dmix_got[0], *[Far(a) for a in dmix_got[1:]], Far(table), Far(q), Far(k), Far(v), Far(mix), Far(pre), params,
        scalars=where, us=21.5, vmem=32,
        scratch=[pltpu.VMEM((span, width), BF)] + [pltpu.VMEM((span, HEAD_DIM), BF)] * 2
        + [pltpu.VMEM((span, width), F32)] * 3,
    )

    ff_all = lax.all_gather(stack_rows(ff_sum, after=[d_qkv]), ("chip", "core"), axis=0, tiled=True)
    grad_gate, grad_up, grad_down = kernel_call(
        functools.partial(ffn_final_kernel, (chips, fsdp, ff, ff_z)),
        [shape_of((rows_z, hidden), F32)] * 2 + [shape_of((hidden // fsdp, model), F32)], Far(ff_all),
    )

    mine, theirs, gain1_part = kernel_call(
        functools.partial(qkv_grad_kernel, fsdp),
        [shape_of((fsdp * half_z, 3 * width), BF)] * 2 + [shape_of((model, 1), F32)],
        Far(n1), d_qkv, Far(w_qkv),
        scalars=where, us=3.0, scratch=[pltpu.VMEM((model, 3 * width), F32)],
    )
    gains = jnp.concatenate([gain1_part, gain2_part], 1).T / params[:2]
    gains = gains.reshape(2, fsdp, rows_z // LANES, LANES).transpose(1, 0, 2, 3)
    gains = jnp.pad(gains, ((0, 0), (0, 0), (0, 2 - rows_z // LANES), (0, 0))).reshape(fsdp, 4, LANES)
    rest = jnp.broadcast_to(small_part[4:], (fsdp, 4, LANES))
    smalls = jnp.concatenate([gains, rest, jnp.zeros((fsdp, PAD - 8, LANES), F32)], 1)
    messages = kernel_call(
        functools.partial(qkv_message_kernel, fsdp),
        [shape_of((half_z + PAD, 3 * width), BF)] * fsdp, mine, pc(theirs), smalls, scalars=where,
    )
    qkv_piece = summed([messages[0]] + [pz(messages[p], p) for p in range(1, fsdp)], 1)[0]
    qkv_same, qkv_places = gather_chips(qkv_piece)
    qkv_other = pc(stack_rows(*qkv_same))
    grad_query, grad_key, grad_value, small_sum = kernel_call(
        functools.partial(qkv_final_kernel, (chips, width, qkv_places, half_z)),
        [shape_of((rows_z, model), F32)] * 3 + [shape_of((PAD, LANES), F32)],
        *qkv_same, qkv_other, scalars=where,
    )
    per = rows_z // LANES
    grad_bias = lax.dynamic_slice(small_sum, (SAME_ROW, depth * heads_z), (2, heads_z)).T
    grad_q_gain = lax.dynamic_slice(small_sum, (Q_ROW, depth * dims_z), (1, dims_z))[0]
    grad_k_gain = lax.dynamic_slice(small_sum, (K_ROW, depth * dims_z), (1, dims_z))[0]

    d_n1 = kernel_call(
        project_back_kernel, [shape_of((chunk, model), BF)] * chips, d_qkv, Far(w_qkv), us=3.0,
        after=[gain1_part],
    )
    dn1_got = exchange(d_n1)
    own_grad, their_grad = kernel_call(
        functools.partial(input_back_kernel, chips),
        [shape_of((slots, model), F32), shape_of((slots, model), BF)],
        Far(x_chunk), Far(d_hidden), params, dn1_got[0], *[Far(a) for a in dn1_got[1:]],
    )
    grad_inputs = by_sequence(own_grad, pc(their_grad).astype(F32))
    return (
        output, grad_inputs, grad_query, grad_key, grad_value, grad_out, grad_gate, grad_up, grad_down,
        small_sum[:per].reshape(-1), small_sum[2 : 2 + per].reshape(-1), grad_bias, grad_q_gain, grad_k_gain,
    )


def solution(mesh):
    ctx, fsdp = mesh.shape["ctx"], mesh.shape["fsdp"]
    chips = ctx // 2
    split = Mesh(mesh.devices.reshape(chips, 2, fsdp), ("chip", "core", "fsdp"))
    rows, row = P("fsdp", None), P("fsdp")
    block, ids = P("fsdp", ("chip", "core"), None), P("fsdp", ("chip", "core"))
    return jax.shard_map(
        functools.partial(layer, chips, fsdp),
        mesh=split,
        in_specs=(block, ids, ids, row) + (rows,) * 7 + (row, row, rows, row, row, block),
        out_specs=(block, block) + (rows,) * 7 + (row, row, rows, row, row),
        check_vma=False,
    )
```

```python
import functools

import jax
import jax.numpy as jnp
import ml_dtypes
import numpy as np
from jax import lax
from jax.experimental import pallas as pl
from jax.experimental.pallas import tpu as pltpu
from jax.sharding import Mesh
from jax.sharding import PartitionSpec as P

EPSILON = 1e-05
ROPE_BASE = 10000.0
NEG_FILL = -1e30
HEAD_DIM = 64
HALF = HEAD_DIM // 2
BF = jnp.bfloat16
F32 = jnp.float32
PAD = 16
LANES = 128
FRONT_US, BACK_US = 0.5, 20.0
PEAK = 3.45e9

NT = (((1,), (1,)), ((), ()))
TN = (((0,), (0,)), ((), ()))
NN = (((1,), (0,)), ((), ()))

Q_ROW, K_ROW, SAME_ROW, OTHER_ROW = 4, 5, 6, 7


def mm(left, right, dims=NN):
    return lax.dot_general(left, right, dims, preferred_element_type=F32)


class Far:
    def __init__(self, *arrays):
        self.arrays = arrays


def kernel_call(kernel, out_shapes, *operands, scalars=None, scratch=(), us=1.0, vmem=40, after=()):
    vmem_spec, any_spec = pl.BlockSpec(memory_space=pltpu.VMEM), pl.BlockSpec(memory_space=pl.ANY)
    arrays, specs, fetched, sources = [], [], [], []
    for operand in operands:
        if isinstance(operand, Far):
            sources.append((len(arrays), len(operand.arrays)))
            arrays += operand.arrays
            specs += [any_spec] * len(operand.arrays)
            first = operand.arrays[0]
            rows = sum(a.shape[0] for a in operand.arrays)
            fetched.append(pltpu.VMEM((rows,) + first.shape[1:], first.dtype))
        else:
            sources.append((len(arrays), 0))
            arrays.append(operand)
            specs.append(vmem_spec)
    far_out = [isinstance(a, Far) for a in out_shapes]
    out_shapes = [a.arrays[0] if isinstance(a, Far) else a for a in out_shapes]
    shipped = [pltpu.VMEM(a.shape, a.dtype) for a, far in zip(out_shapes, far_out) if far]
    n_arrays, n_out, n_own, n_fetched = len(arrays), len(out_shapes), len(scratch), len(fetched)
    n_sems = sum(count for _, count in sources) + len(shipped)
    sems = [pltpu.SemaphoreType.DMA((n_sems,))] if n_sems else []
    head_specs = [] if scalars is None else [pl.BlockSpec(memory_space=pltpu.SMEM)]
    head_arrays = [] if scalars is None else [scalars]
    n_head = len(head_arrays)

    def whole(*refs):
        head, refs = refs[:n_head], refs[n_head:]
        given, refs = refs[:n_arrays], refs[n_arrays + len(after) :]
        outs, refs = list(refs[:n_out]), refs[n_out:]
        own, refs = refs[:n_own], refs[n_own:]
        local, refs = refs[:n_fetched], refs[n_fetched:]
        sem, at, copies, ins = (refs[-1] if n_sems else None), 0, [], []
        for first, count in sources:
            if not count:
                ins.append(given[first])
                continue
            target, local = local[0], local[1:]
            row = 0
            for ref in given[first : first + count]:
                part = target if count == 1 else target.at[pl.ds(row, ref.shape[0])]
                row += ref.shape[0]
                copies.append(pltpu.make_async_copy(ref, part, sem.at[at]))
                copies[-1].start()
                at += 1
            ins.append(target)
        ship, waits = [], []
        for n in range(n_out):
            if far_out[n]:

                def start(source=refs[len(ship)], target=outs[n], at=at + len(ship), started=[]):
                    if not started:
                        started.append(pltpu.make_async_copy(source, target, sem.at[at]))
                        started[0].start()
                        waits.append(started[0])

                outs[n] = refs[len(ship)]
                ship.append(start)
        for copy in copies:
            copy.wait()
        extra = {"ship": ship} if ship else {}
        outs[-1][...] = jnp.zeros(outs[-1].shape, F32)
        kernel(*head, *ins, *outs[:-1], *own, **extra)
        for start in ship:
            start()
        for copy in waits:
            copy.wait()

    return pl.pallas_call(
        whole,
        out_shape=out_shapes,
        in_specs=head_specs + specs + [any_spec] * len(after),
        out_specs=[any_spec if far else vmem_spec for far in far_out],
        scratch_shapes=list(scratch) + fetched + shipped + sems,
        cost_estimate=pl.CostEstimate(flops=int(us * PEAK), bytes_accessed=0, transcendentals=0),
        compiler_params=pltpu.CompilerParams(vmem_limit_bytes=vmem * 2**20),
    )(*head_arrays, *arrays, *after)


def shape_of(dims, dtype):
    return jax.ShapeDtypeStruct(tuple(dims), dtype)


def place():
    return lax.axis_index("core"), lax.axis_index("chip"), lax.axis_index("fsdp")


def stack_kernel(counts, *refs):
    at = 0
    for ref, count in zip(refs[:-1], counts):
        refs[-1][pl.ds(at, count), :] = ref[pl.ds(0, count), :]
        at += count


def lane_of(shape):
    return lax.broadcasted_iota(jnp.int32, shape, 1)


def head_sum(values):
    row = lax.broadcasted_iota(jnp.int32, (LANES, LANES), 0) // HEAD_DIM
    col = lax.broadcasted_iota(jnp.int32, (LANES, LANES), 1) // HEAD_DIM
    ones = (row == col).astype(BF)
    high = values.astype(BF)
    low = (values - high.astype(F32)).astype(BF)
    return mm(high, ones) + mm(low, ones)


def row_totals(values):
    ones = jnp.ones((8, values.shape[1]), BF)
    high = values.astype(BF)
    low = (values - high.astype(F32)).astype(BF)
    return (mm(ones, high, NT) + mm(ones, low, NT))[:1]


def half_swap(values):
    first = lane_of(values.shape) % HEAD_DIM < HALF
    return jnp.where(first, pltpu.roll(values, LANES - HALF, 1), pltpu.roll(values, HALF, 1))


def rotary(table):
    lane = lane_of(table.shape)
    base = jnp.where(lane < HEAD_DIM, table, pltpu.roll(table, HEAD_DIM, 1))
    other = half_swap(base)
    first = lane % HEAD_DIM < HALF
    return jnp.where(first, base, other), jnp.where(first, -other, base)


def one_lane(row, index):
    return jnp.sum(jnp.where(lane_of(row.shape) == index, row, 0.0), axis=1, keepdims=True)


def key_features(kind, params, head):
    same = one_lane(params[SAME_ROW : SAME_ROW + 1, :LANES], head)
    other = one_lane(params[OTHER_ROW : OTHER_ROW + 1, :LANES], head)
    return jnp.where(kind == 0.0, other, jnp.where(kind == 1.0, same, NEG_FILL)).astype(BF)


def scale_of(x):
    return lax.rsqrt(jnp.mean(x * x, axis=-1, keepdims=True) + EPSILON)


def norm_back(grad, x, gain):
    scale = scale_of(x)
    unit = x * scale
    scaled = grad * gain
    return scale * (scaled - unit * jnp.mean(scaled * unit, axis=-1, keepdims=True))


def input_kernel(inputs, times, variates, cotangent, own, other):
    slots = inputs.shape[1]
    core = lax.axis_index("core")
    for index, out in ((core, own), (1 - core, other)):
        out[pl.ds(0, slots), :] = inputs[index]
        time, variate = times[pl.ds(index, 1), :], variates[pl.ds(index, 1), :]
        rows = [time >> 8, time & 255, variate, jnp.zeros((PAD - 3, slots), jnp.int32)]
        out[pl.ds(slots, PAD), :] = jnp.zeros((PAD, out.shape[1]), BF)
        out[pl.ds(slots, PAD), pl.ds(0, slots)] = jnp.concatenate(rows, 0).astype(F32).astype(BF)
        out[pl.ds(slots + PAD, slots), :] = cotangent[index]


def halves_kernel(at, own, other, out):
    count = out.shape[0] // 2
    out[pl.ds(0, count), :] = own[pl.ds(at, count), :]
    out[pl.ds(count, count), :] = other[pl.ds(at, count), :]


def cut_kernel(side, up, first, second):
    cut = first.shape[0]
    first[...] = side[pl.ds(0, cut), :]
    second[...] = up[pl.ds(cut, second.shape[0]), :]


def weight_kernel(width, w_query, w_key, w_value, out):
    core, chip, _ = place()
    half = w_query.shape[0] // 2
    at = 0
    for ref in (w_query, w_key, w_value):
        for n in range(width // LANES):
            col = pl.multiple_of(chip * width + n * LANES, LANES)
            row = pl.multiple_of(core * half, 16)
            out[pl.ds(at, half), :] = ref[pl.ds(row, half), pl.ds(col, LANES)]
            at += half


def small_kernel(w_out, gain_attn, gain_ffn, head_bias, q_gain, k_gain, out):
    depth = lax.axis_index("fsdp")
    piece = w_out.shape[0]
    if out.shape[0] > piece + PAD:
        out[...] = jnp.zeros(out.shape, BF)
    out[pl.ds(0, piece), :] = w_out[...]
    lane = lane_of((1, LANES))
    rows = [gain_attn[...].astype(F32), gain_ffn[...].astype(F32)]
    rows = [jnp.concatenate([r, jnp.zeros((2 - r.shape[0], LANES), F32)], 0) if r.shape[0] < 2 else r for r in rows]
    for ref in (q_gain, k_gain):
        value, dims = ref[...].astype(F32), ref.shape[1]
        row = jnp.zeros((1, LANES), F32)
        for j in range(dims):
            row = jnp.where(lane % HEAD_DIM == depth * dims + j, value[:, j : j + 1], row)
        rows.append(row)
    value, heads = head_bias[...].astype(F32), head_bias.shape[0]
    for n in range(2):
        row = jnp.zeros((1, LANES), F32)
        for j in range(heads):
            row = jnp.where(lane == depth * heads + j, value[j : j + 1, n : n + 1], row)
        rows.append(row)
    rows.append(jnp.zeros((PAD - 8, LANES), F32))
    at = out.shape[0] - PAD
    out[pl.ds(at, PAD), :] = jnp.zeros((PAD, out.shape[1]), BF)
    out[pl.ds(at, PAD), pl.ds(0, LANES)] = jnp.concatenate(rows, 0).astype(BF)


def params_kernel(depths, pieces, z_out, params):
    depth = lax.axis_index("fsdp")
    count = pieces.shape[0] // depths
    piece = z_out.shape[0] // depths
    rows_z = params.shape[1] // depths
    params[...] = jnp.zeros_like(params)
    total = None
    for p in range(depths):
        z_out[pl.ds(p * piece, piece), :] = pieces[pl.ds(p * count, piece), :]
        small = pieces[pl.ds((p + 1) * count - PAD, PAD), pl.ds(0, LANES)].astype(F32)
        total = small if total is None else total + small
        for n in range(rows_z // LANES):
            col = pl.multiple_of((depth ^ p) * rows_z + n * LANES, LANES)
            params[pl.ds(0, 1), pl.ds(col, LANES)] = small[n : n + 1]
            params[pl.ds(1, 1), pl.ds(col, LANES)] = small[2 + n : 3 + n]
    for n in (Q_ROW, K_ROW, SAME_ROW, OTHER_ROW):
        params[pl.ds(n, 1), pl.ds(0, LANES)] = total[n : n + 1]


def turn_table(span):
    coarse = -(-span // 16)
    frequency = ROPE_BASE ** (-np.arange(HALF) * (2.0 / HEAD_DIM))
    steps = np.concatenate([16.0 * np.arange(coarse), np.arange(16.0)])
    angles = steps[:, None] * frequency
    exact = np.concatenate([np.cos(angles), np.sin(angles)], axis=1).astype(np.float32)
    parts, rest = [], exact
    for _ in range(3):
        low = rest.astype(ml_dtypes.bfloat16)
        parts.append(low)
        rest = rest - low.astype(np.float32)
    return np.concatenate(parts, axis=1)


def slot_table(lengths, ids, turns, slots, d):
    tables = []
    coarse = turns.shape[0] - 16
    for c in range(2):
        rows = ids[c][:, :slots].astype(F32)
        high, low, variate = rows[0:1].astype(jnp.int32), rows[1:2].astype(jnp.int32), rows[2:3].astype(jnp.int32)
        time = high * 256 + low
        index = lax.broadcasted_iota(jnp.int32, (coarse, slots), 0)
        hot_a = jnp.where(index == time >> 4, 1.0, 0.0).astype(BF)
        index = lax.broadcasted_iota(jnp.int32, (16, slots), 0)
        hot_b = jnp.where(index == (time & 15), 1.0, 0.0).astype(BF)
        turn_a, turn_b = mm(hot_a, turns[:coarse], TN), mm(hot_b, turns[coarse:], TN)
        turn_a = turn_a[:, :64] + turn_a[:, 64:128] + turn_a[:, 128:]
        turn_b = turn_b[:, :64] + turn_b[:, 64:128] + turn_b[:, 128:]
        cos_a, sin_a, cos_b, sin_b = turn_a[:, :HALF], turn_a[:, HALF:], turn_b[:, :HALF], turn_b[:, HALF:]
        index = lax.broadcasted_iota(jnp.int32, (HEAD_DIM, slots), 0)
        hot = jnp.where(index == variate, 1.0, 0.0).astype(BF)
        eye = lax.broadcasted_iota(jnp.int32, (HEAD_DIM, HEAD_DIM), 0) == lane_of((HEAD_DIM, HEAD_DIM))
        kind = mm(hot, jnp.where(eye, 1.0, 0.0).astype(BF), TN)
        tables.append(jnp.concatenate([cos_a * cos_b - sin_a * sin_b, sin_a * cos_b + cos_a * sin_b, kind], axis=1))
    table = jnp.concatenate(tables, axis=0)
    hidden = jnp.logical_and(lane_of(table.shape) >= HEAD_DIM, jnp.logical_not(valid_rows(lengths, 2, slots, d)))
    return jnp.where(hidden, 2.0, table)


def norm_kernel(chips, lengths, xs, turns, params, n1, tables, kinds, hots):
    chunk = n1.shape[0] // chips
    slots = chunk // 2
    for d in range(chips):
        rows = pl.ds(d * chunk, chunk)
        x = xs[pl.ds(d * (chunk + 2 * PAD), chunk + 2 * PAD), :]
        ids = [x[slots : slots + PAD], x[2 * slots + PAD :]]
        table = slot_table(lengths, ids, turns[...], slots, d)
        tables[rows, :] = table
        kind = table[:, HEAD_DIM:]
        kinds[rows, :] = kind.astype(BF)
        hots[rows, :] = (kind == 1.0).astype(BF)
        x = jnp.concatenate([x[:slots], x[slots + PAD : 2 * slots + PAD]], axis=0).astype(F32)
        n1[rows, :] = (x * scale_of(x) * params[pl.ds(0, 1), :]).astype(BF)


def attend_kernel(cfg, packed, n1, tables, kinds, hots, params, *refs, ship):
    chips, heads, depths = cfg
    q, k, v, pre, w, mix = refs[:6]
    lows = refs[6:]
    span, width = q.shape
    chunk = span // chips
    half = n1.shape[1] // depths // 2
    blocks = w.shape[1] // LANES
    for b in range(2 * depths):
        for n in range(blocks):
            w[pl.ds(b * half, half), pl.ds(n * LANES, LANES)] = packed[pl.ds((b * blocks + n) * half, half), :]
    ship[4]()
    for d in range(chips):
        rows = pl.ds(d * chunk, chunk)
        cosine, sine = rotary(tables[rows, :])
        both = mm(n1[rows, :], w[...])
        v[rows, :] = both[:, 2 * width :].astype(BF)
        pre[rows, :] = both[:, : 2 * width]
        for source, row, target in ((0, Q_ROW, q), (width, K_ROW, k)):
            gain = params[pl.ds(row, 1), pl.ds(0, LANES)]
            for g in range(width // LANES):
                value = both[:, source + LANES * g : source + LANES * (g + 1)]
                scale = lax.rsqrt(head_sum(value * value) * (1.0 / HEAD_DIM) + EPSILON)
                normed = value * scale * gain
                target[rows, pl.ds(LANES * g, LANES)] = (normed * cosine + half_swap(normed) * sine).astype(BF)
    for n in range(4):
        ship[n]()
    for h in range(heads):
        lanes = pl.ds(HEAD_DIM * h, HEAD_DIM)
        features = key_features(kinds[...].astype(F32), params, lax.axis_index("chip") * heads + h)
        keys = jnp.concatenate([k[:, lanes], features], axis=1)
        values = v[:, lanes]
        for d in range(chips):
            rows = pl.ds(d * chunk, chunk)
            query = jnp.concatenate([q[rows, lanes] * BF(0.125), hots[rows, :]], axis=1)
            terms = jnp.exp(mm(query, keys, NT))
            denom = jnp.sum(terms, axis=-1, keepdims=True)
            part = mm(terms.astype(BF), values) / denom
            mix[rows, lanes] = part
            lows[d][:, lanes] = part.astype(BF)


def mix_out_kernel(width, chips, own, w_out, params, *refs):
    pieces, (h_ref, n2) = refs[:chips], refs[chips:]
    chunk = h_ref.shape[0]
    slots = chunk // 2
    total = None
    for d in range(chips):
        row = pl.multiple_of((lax.axis_index("chip") ^ d) * width, LANES)
        term = mm(pieces[d][...], w_out[pl.ds(row, width), :])
        total = term if total is None else total + term
    x = jnp.concatenate([own[pl.ds(0, slots), :], own[pl.ds(slots + PAD, slots), :]], axis=0)
    h = x.astype(F32) + total
    h_ref[...] = h
    n2[...] = (h * scale_of(h) * params[pl.ds(1, 1), :]).astype(BF)


def valid_rows(lengths, halves, slots, d):
    core, chip, _ = place()
    row = lax.broadcasted_iota(jnp.int32, (slots, 1), 0)
    here = 2 * chip + core
    return jnp.concatenate([(here ^ (2 * d + c)) * slots + row < lengths[core] for c in range(halves)], axis=0)


def pack_kernel(cfg, w_gate, w_up, w_down, packed):
    chips, depths, ff, ff_z = cfg
    half, hidden = w_gate.shape[0] // 2, w_gate.shape[1]
    model = w_down.shape[1]
    blocks = -(-2 * ff // LANES)
    padded = -(-ff_z // 16) * 16
    quarters = model // 2 // LANES
    core, chip, _ = place()
    rows = pl.ds(pl.multiple_of(core * half, 16), half)
    for t in range(chips):

        @pl.when(chip == t)
        def _():
            parts = []
            for ref in (w_gate, w_up):
                both = ref[rows, :]
                parts += [both[:, n * (hidden // depths) + t * ff_z :][:, :ff_z] for n in range(depths)]
            if 2 * ff % LANES:
                parts.append(jnp.zeros((half, blocks * LANES - 2 * ff), BF))
            tight = jnp.concatenate(parts, axis=1)
            for n in range(blocks):
                packed[pl.ds(n * half, half), :] = tight[:, n * LANES : (n + 1) * LANES]
            for n in range(quarters):
                col = pl.multiple_of(core * (model // 2) + n * LANES, LANES)
                value = w_down[pl.ds(t * ff_z, ff_z), pl.ds(col, LANES)]
                if padded > ff_z:
                    value = jnp.concatenate([value, jnp.zeros((padded - ff_z, LANES), BF)], axis=0)
                packed[pl.ds(blocks * half + n * padded, padded), :] = value


def unpack_kernel(cfg, packed, w_gu, w_d):
    depths, ff, ff_z, ff_pad = cfg
    model = w_gu.shape[0]
    half = model // depths // 2
    blocks = -(-2 * ff // LANES)
    padded = -(-ff_z // 16) * 16
    quarters = model // 2 // LANES
    piece = blocks * half + quarters * padded
    w_gu[...] = jnp.zeros_like(w_gu)
    w_d[...] = jnp.zeros_like(w_d)
    for z in range(depths):
        for c in range(2):
            base = (2 * z + c) * piece
            rows = pl.ds((2 * z + c) * half, half)
            both = jnp.concatenate([packed[pl.ds(base + n * half, half), :] for n in range(blocks)], axis=1)
            w_gu[rows, pl.ds(0, ff)] = both[:, :ff]
            w_gu[rows, pl.ds(ff_pad, ff)] = both[:, ff : 2 * ff]
            for n in range(quarters):
                at = base + blocks * half + n * padded
                w_d[pl.ds(z * ff_z, ff_z), pl.ds(c * model // 2 + n * LANES, LANES)] = packed[pl.ds(at, ff_z), :]


def ffn_kernel(cfg, lengths, n2, dy, w_gu, w_d, dn2, act, dgu):
    d, ff_pad = cfg
    n2 = n2[...]
    dy = jnp.where(valid_rows(lengths, 2, n2.shape[0] // 2, d), dy[...], jnp.zeros_like(n2))
    pre = mm(n2, w_gu[...])
    gate, up = pre[:, :ff_pad], pre[:, ff_pad:]
    sig = jax.nn.sigmoid(gate)
    silu = gate * sig
    low = (silu * up).astype(BF)
    act[...] = low
    d_act = mm(dy, w_d[...], NT)
    d_up = (d_act * silu).astype(BF)
    d_gate = (d_act * up * sig * (1.0 + gate * (1.0 - sig))).astype(BF)
    both = jnp.concatenate([d_gate, d_up], axis=1)
    dgu[...] = both
    dn2[...] = mm(both, w_gu[...], NT).astype(BF)


def down_kernel(places, w_d, *refs):
    acts, outs = refs[: len(places)], refs[len(places) :]
    for act, (n, row) in zip(acts, places):
        outs[n][pl.ds(row, act.shape[0]), :] = mm(act[...], w_d[...]).astype(BF)


def core_sum_kernel(places, mine, got, *outs):
    depths, piece = mine.shape[1:3]
    for d, (n, row) in enumerate(places):
        for p in range(depths):
            total = mine[d, p].astype(F32) + got[d, p].astype(F32)
            outs[n][pl.ds(row + p * piece, piece), :] = total.astype(BF)


def half_sum_kernel(keep, got, own, send):
    rows = own.shape[0]
    total = (keep[...].astype(F32) + got[...].astype(F32)).astype(BF)
    own[...] = total[:rows]
    send[...] = total[rows:]


def ffn_grad_kernel(cfg, lengths, n2, dy, act, dgu, w_gu, params, packed, gain2):
    chips, depths, ff, ff_z, ff_pad = cfg
    model = w_gu.shape[0]
    chunk = n2.shape[0] // chips
    for d in range(chips):
        rows = pl.ds(d * chunk, chunk)
        part = dy[rows, :]
        dy[rows, :] = jnp.where(valid_rows(lengths, 2, chunk // 2, d), part, jnp.zeros_like(part))
    half = model // depths // 2
    blocks = -(-2 * ff // LANES)
    padded = -(-ff_z // 16) * 16
    quarters = model // 2 // LANES
    piece = blocks * half + quarters * padded
    for b in range(2 * depths):
        rows = pl.ds(b * half, half)
        grad = mm(n2[:, rows], dgu[...], TN)
        gain = params[pl.ds(1, 1), rows]
        gain2[pl.ds(0, 1), rows] = row_totals(grad * w_gu[rows, :].astype(F32)) / gain
        tight = jnp.concatenate([grad[:, :ff], grad[:, ff_pad : ff_pad + ff]], axis=1).astype(BF)
        if 2 * ff % LANES:
            tight = jnp.concatenate([tight, jnp.zeros((half, blocks * LANES - 2 * ff), BF)], axis=1)
        for n in range(blocks):
            packed[pl.ds(b * piece + n * half, half), :] = tight[:, n * LANES : (n + 1) * LANES]
    for z in range(depths):
        grad = mm(act[:, pl.ds(z * ff_z, ff_z)], dy[...], TN).astype(BF)
        if padded > ff_z:
            grad = jnp.concatenate([grad, jnp.zeros((padded - ff_z, model), BF)], axis=0)
        for c in range(2):
            for n in range(quarters):
                at = (2 * z + c) * piece + blocks * half + n * padded
                col = c * model // 2 + n * LANES
                packed[pl.ds(at, padded), :] = grad[:, col : col + LANES]


def ffn_final_kernel(cfg, packed, g_gate, g_up, g_down):
    chips, depths, ff, ff_z = cfg
    model = g_down.shape[1]
    half = model // depths // 2
    hidden_z = chips * ff_z
    blocks = -(-2 * ff // LANES)
    padded = -(-ff_z // 16) * 16
    quarters = model // 2 // LANES
    piece = blocks * half + quarters * padded
    for t in range(chips):
        for c in range(2):
            base = (2 * t + c) * piece
            both = jnp.concatenate([packed[pl.ds(base + n * half, half), :] for n in range(blocks)], axis=1).astype(F32)
            for z in range(depths):
                cols = pl.ds(z * hidden_z + t * ff_z, ff_z)
                g_gate[pl.ds(c * half, half), cols] = both[:, z * ff_z : (z + 1) * ff_z]
                g_up[pl.ds(c * half, half), cols] = both[:, ff + z * ff_z : ff + (z + 1) * ff_z]
            for n in range(quarters):
                at = base + blocks * half + n * padded
                rows = pl.ds(t * ff_z, ff_z)
                g_down[rows, pl.ds(c * model // 2 + n * LANES, LANES)] = packed[pl.ds(at, ff_z), :].astype(F32)


def output_kernel(count, lengths, h, *refs):
    terms, (out, low) = refs[:count], refs[count:]
    slots = out.shape[0]
    total = h[...]
    for ref in terms:
        total = total + ref[...].astype(F32)
    total = jnp.where(valid_rows(lengths, 2, slots, 0), total, 0.0).astype(BF)
    out[...] = total[:slots]
    low[...] = total[slots:]


def hidden_back_kernel(width, chips, lengths, h, dy, params, w_out, *refs):
    terms, (d_h, d_low), d_mix = refs[:chips], refs[chips : chips + 2], refs[chips + 2 :]
    grad = terms[0][...].astype(F32)
    for ref in terms[1:]:
        grad = grad + ref[...].astype(F32)
    own = jnp.where(valid_rows(lengths, 2, dy.shape[0] // 2, 0), dy[...].astype(F32), 0.0)
    total = own + norm_back(grad, h[...], params[pl.ds(1, 1), :])
    d_h[...] = total
    low = total.astype(BF)
    d_low[...] = low
    for d in range(chips):
        row = pl.multiple_of((lax.axis_index("chip") ^ d) * width, LANES)
        d_mix[d][...] = mm(low, w_out[pl.ds(row, width), :], NT).astype(BF)


def out_grad_kernel(cfg, d_low, *refs):
    chips, depths, width, piece = cfg
    mixes, (mine, theirs, full) = refs[:chips], refs[chips:]
    core, chip, depth = place()
    rows_z = full.shape[0] // depths
    for d in range(chips):
        row = pl.multiple_of((chip ^ d) * width, LANES)
        full[pl.ds(row, width), :] = mm(mixes[d][...], d_low[...], TN)
    for out, c in ((mine, core), (theirs, 1 - core)):
        for d in range(chips):
            for p in range(depths):
                row = (depth ^ p) * rows_z + c * (rows_z // 2) + (chip ^ d) * piece
                out[d, p] = full[pl.ds(pl.multiple_of(row, 8), piece), :].astype(BF)


def sum_kernel(*refs):
    total = refs[0][...].astype(F32)
    for ref in refs[1:-1]:
        total = total + ref[...].astype(F32)
    refs[-1][...] = total.astype(BF)


def input_back_kernel(chips, own_x, d_h, params, *refs):
    terms, (out, low) = refs[:chips], refs[chips:]
    slots = out.shape[0]
    grad = terms[0][...].astype(F32)
    for ref in terms[1:]:
        grad = grad + ref[...].astype(F32)
    x = jnp.concatenate([own_x[pl.ds(0, slots), :], own_x[pl.ds(slots + PAD, slots), :]], axis=0).astype(F32)
    total = d_h[...] + norm_back(grad, x, params[pl.ds(0, 1), :])
    out[...] = total[:slots]
    low[...] = total[slots:].astype(BF)


def by_sequence_kernel(result, their_result, grad_x, their_grad, out, grad):
    core = lax.axis_index("core")
    out[core] = result[...]
    out[1 - core] = their_result[...]
    grad[core] = grad_x[...]
    grad[1 - core] = their_grad[...].astype(F32)


def attend_back_kernel(cfg, *refs):
    chips, heads, width = cfg
    dmix, tables, q, k, v, mix, pre, params, d_qkv, smalls = refs[:10]
    kinds, hots, dq_scr, dk_scr, dv_scr = refs[10:]
    span = k.shape[0]
    chunk = span // chips
    dk_scr[...] = jnp.zeros_like(dk_scr)
    dv_scr[...] = jnp.zeros_like(dv_scr)
    smalls[...] = jnp.zeros_like(smalls)
    for d in range(chips):
        rows = pl.ds(d * chunk, chunk)
        kind = tables[rows, HEAD_DIM:]
        kinds[rows, :] = kind.astype(BF)
        hots[rows, :] = (kind == 1.0).astype(BF)
    lane = lane_of((1, LANES))

    def step(c, carry):
        part = pl.ds(pl.multiple_of(c * chunk, chunk), chunk)
        query_hot = hots[part, :]
        for h in range(heads):
            lanes = pl.ds(HEAD_DIM * h, HEAD_DIM)
            key = k[:, lanes]
            index = lax.axis_index("chip") * heads + h
            keys = jnp.concatenate([key, key_features(kinds[...].astype(F32), params, index)], axis=1)
            query = q[part, lanes] * BF(0.125)
            grad = dmix[part, lanes]
            product = mix[part, lanes] * grad.astype(F32)
            high = product.astype(BF)
            low = (product - high.astype(F32)).astype(BF)
            ones = jnp.ones((8, HEAD_DIM), BF)
            delta = (mm(ones, high, NT) + mm(ones, low, NT))[:1]
            terms = jnp.exp(mm(keys, jnp.concatenate([query, query_hot], axis=1), NT))
            prob = terms * (1.0 / jnp.sum(terms, axis=0, keepdims=True))
            d_score = (prob * (mm(v[:, lanes], grad, NT) - delta)).astype(BF)
            dk_scr[:, lanes] += mm(d_score, query)
            dv_scr[:, lanes] += mm(prob.astype(BF), grad)
            both = mm(d_score, jnp.concatenate([key, hots[...]], axis=1), TN)
            dq_scr[part, lanes] = both[:, :HEAD_DIM] * 0.125
            pairs = both[:, HEAD_DIM:]
            hot = query_hot.astype(F32)
            for row, weight in ((SAME_ROW, hot), (OTHER_ROW, 1.0 - hot)):
                value = jnp.sum(jnp.sum(pairs * weight, axis=0, keepdims=True), axis=1, keepdims=True)
                smalls[pl.ds(row, 1), :] += jnp.where(lane == index, value, 0.0)
        return carry

    lax.fori_loop(0, chips, step, 0)
    for d in range(chips):
        part = pl.ds(d * chunk, chunk)
        cosine, sine = rotary(tables[part, :])
        for n, (grads, row) in enumerate(((dq_scr, Q_ROW), (dk_scr, K_ROW))):
            gain = params[pl.ds(row, 1), pl.ds(0, LANES)]
            for g in range(width // LANES):
                grad = grads[part, pl.ds(LANES * g, LANES)]
                value = pre[part, pl.ds(n * width + LANES * g, LANES)]
                scale = lax.rsqrt(head_sum(value * value) * (1.0 / HEAD_DIM) + EPSILON)
                unit = value * scale
                d_normed = grad * cosine - half_swap(grad) * sine
                total = jnp.sum(d_normed * unit, axis=0, keepdims=True)
                smalls[pl.ds(row, 1), :] += total + pltpu.roll(total, HEAD_DIM, 1)
                scaled = d_normed * gain
                mean = head_sum(scaled * unit) * (1.0 / HEAD_DIM)
                d_qkv[part, pl.ds(n * width + LANES * g, LANES)] = (scale * (scaled - unit * mean)).astype(BF)
        d_qkv[part, pl.ds(2 * width, width)] = dv_scr[part, :].astype(BF)


def qkv_grad_kernel(depths, n1, d_qkv, w, params, mine, theirs, gain1, full):
    core, _, depth = place()
    model = n1.shape[1]
    half = model // depths // 2
    tile = 256
    for n in range(model // tile):
        rows = pl.ds(n * tile, tile)
        grad = mm(n1[:, rows], d_qkv[...], TN)
        full[rows, :] = grad
        gain1[pl.ds(0, 1), rows] = row_totals(grad * w[rows, :].astype(F32)) / params[pl.ds(0, 1), rows]
    for out, c in ((mine, core), (theirs, 1 - core)):
        for p in range(depths):
            row = pl.multiple_of((2 * (depth ^ p) + c) * half, 16)
            out[pl.ds(p * half, half), :] = full[pl.ds(row, half), :].astype(BF)


def project_back_kernel(d_qkv, w, *outs):
    chunk = outs[0].shape[0]
    for n, out in enumerate(outs):
        out[...] = mm(d_qkv[pl.ds(n * chunk, chunk), :], w[...], NT).astype(BF)


def message_kernel(cfg, mine, got, gain1, gain2, small, *refs):
    depths, count = cfg
    parts, outs = refs[:count], refs[count:]
    half = mine.shape[0] // depths
    blocks = mine.shape[1] // LANES
    per = 2 * half // LANES
    for p, out in enumerate(outs):
        rows = pl.ds(p * half, half)
        both = (mine[rows, :].astype(F32) + got[rows, :].astype(F32)).astype(BF)
        for n in range(blocks):
            out[pl.ds(n * half, half), :] = both[:, n * LANES : (n + 1) * LANES]
        layer_rows = []
        for ref in (gain1, gain2):
            for n in range(2):
                col = pl.multiple_of((lax.axis_index("fsdp") ^ p) * 2 * half + n * LANES, LANES)
                layer_rows.append(ref[pl.ds(0, 1), pl.ds(col, LANES)] if n < per else jnp.zeros((1, LANES), F32))
        block = jnp.concatenate(layer_rows + [small[pl.ds(4, 4), :], jnp.zeros((PAD - 8, LANES), F32)], axis=0)
        at = blocks * half
        out[pl.ds(at, PAD), :] = block.astype(BF)
        piece = parts[0].shape[0] // depths
        rows = pl.ds(p * piece, piece)
        total = parts[0][rows, :].astype(F32)
        for ref in parts[1:]:
            total = total + ref[rows, :].astype(F32)
        total = total.astype(BF)
        for n in range(total.shape[1] // LANES):
            out[pl.ds(at + PAD + n * piece, piece), :] = total[:, n * LANES : (n + 1) * LANES]


def projections_final_kernel(cfg, same, other, g_q, g_k, g_v, g_o, smalls):
    chips, width, half, piece = cfg
    core, chip, _ = place()
    model = g_q.shape[1]
    per = width // LANES
    blocks = 3 * per
    count = blocks * half + PAD + model // LANES * piece
    total = None
    for c in range(2):
        half_of = core if c == 0 else 1 - core
        row = pl.multiple_of(half_of * half, 16)
        for d in range(chips):
            value = (same if c == 0 else other)[pl.ds(d * count, count), :]
            for n, out in enumerate((g_q, g_k, g_v)):
                for m in range(per):
                    col = pl.multiple_of((chip ^ d) * width + m * LANES, LANES)
                    at = (n * per + m) * half
                    out[pl.ds(row, half), pl.ds(col, LANES)] = value[at : at + half].astype(F32)
            at = blocks * half
            small = value[at : at + PAD].astype(F32)
            total = small if total is None else total + small
            out_row = pl.multiple_of(half_of * half + (chip ^ d) * piece, 8)
            for n in range(model // LANES):
                start = at + PAD + n * piece
                g_o[pl.ds(out_row, piece), pl.ds(n * LANES, LANES)] = value[start : start + piece].astype(F32)
    smalls[...] = total


def w_out_kernel(cfg, same, other, out, full):
    chips, depths, piece = cfg
    core, chip, depth = place()
    here = 2 * chip + core
    rows_z = out.shape[0] // depths
    for c in range(2):
        for d in range(chips):
            value = (same if c == 0 else other)[pl.ds(d * depths * piece, depths * piece), :].astype(F32)
            for p in range(depths):
                row = (depth ^ p) * rows_z + (here ^ (2 * d + c)) * piece
                full[pl.ds(pl.multiple_of(row, 8), piece), :] = value[p * piece : (p + 1) * piece]
    out[...] = full[...].astype(BF)


def layer(
    chips, fsdp, inputs, time_ids, variate_ids, seq_lengths, w_query, w_key, w_value, w_out, w_gate,
    w_up, w_down, gain_attn, gain_ffn, head_bias, q_gain, k_gain, cotangent,
):
    _, slots, model = inputs.shape
    heads = model // HEAD_DIM // chips
    width = heads * HEAD_DIM
    rows_z = w_query.shape[0]
    half_z = rows_z // 2
    hidden = w_gate.shape[1]
    ff = hidden // chips
    ff_z = ff // fsdp
    ff_pad = -(-ff // 256) * 256
    chunk = 2 * slots
    span = chips * chunk
    core, chip, depth = lax.axis_index("core"), lax.axis_index("chip"), lax.axis_index("fsdp")
    here = 2 * chip + core
    heads_z, dims_z = head_bias.shape[0], q_gain.shape[0]
    last = []

    def step(kernel, cfg, out_shapes, *operands, after=(), **options):
        if cfg is not None:
            kernel = functools.partial(kernel, cfg)
        token = shape_of((8, LANES), F32)
        outs = kernel_call(kernel, out_shapes + [token], *operands, after=last[-1:] + list(after), **options)
        last.append(outs[-1])
        return outs[:-1]

    def pc(a):
        return lax.ppermute(a, "core", [(0, 1), (1, 0)])

    def pt(a, p):
        return lax.ppermute(a, "chip", [(n, n ^ p) for n in range(chips)])

    def pz(a, p):
        return lax.ppermute(a, "fsdp", [(n, n ^ p) for n in range(fsdp)])

    def stack(*parts, rows=None, after=()):
        counts = [rows or a.shape[0] for a in parts]
        out = shape_of((sum(counts), parts[0].shape[1]), BF)
        return step(stack_kernel, counts, [out], *[Far(a) for a in parts], us=0.6, after=after)[0]

    def gather_first(own):
        if chips == 4:
            return [own, pt(own, 1), pt(own, 2)]
        return [own] + [pt(own, d) for d in range(1, chips)]

    def gather_second(got):
        if chips != 4:
            return [[a] for a in got]
        rows, cols = got[0].shape
        cut = rows // 32 * 16
        first, second = step(
            cut_kernel, None, [shape_of((cut, cols), BF), shape_of((rows - cut, cols), BF)],
            Far(got[1]), Far(got[2]), us=0.8,
        )
        return [[a] for a in got] + [[pt(first, 2), pt(second, 1)]]

    def exchange(parts):
        return [parts[0]] + [pt(parts[d], d) for d in range(1, chips)]

    def scatter_layout(rows, axis):
        if chips != 4:
            return [(d, 0) for d in range(chips)], [rows] * chips
        cross = (1, 3) if axis == 1 else (2, 3)
        near = (0, 2) if axis == 1 else (0, 1)
        return [(1, cross.index(d) * rows) if d in cross else (0, near.index(d) * rows) for d in range(4)], [2 * rows] * 2

    def scatter_first(parts, axis):
        if chips != 4:
            return exchange(parts)
        return [parts[0], pt(parts[1], axis)]

    def scatter_second(got, axis):
        if chips != 4:
            return got
        rows, cols = got[0].shape
        own, send = step(half_sum_kernel, None, [shape_of((rows // 2, cols), BF)] * 2, *far(got), us=0.3)
        return [own, pt(send, 3 - axis)]

    def far(arrays):
        return [Far(a) for a in arrays]

    def joined(lists):
        return Far(*[a for part in lists for a in part])

    blocks = 3 * width // LANES
    body = blocks * half_z
    own_qkv = step(
        weight_kernel, width, [shape_of((body, LANES), BF)], Far(w_query), Far(w_key), Far(w_value), us=1.5
    )[0]
    packed_qkv = lax.all_gather(own_qkv, ("fsdp", "core"), axis=0, tiled=True)

    own_in, other_in = step(
        input_kernel, None, [shape_of((2 * slots + PAD, model), BF)] * 2,
        Far(inputs), time_ids, variate_ids, Far(cotangent), us=1.0,
    )
    got_in = pc(other_in)
    piece = rows_z // (2 * chips)
    own_out = step(
        small_kernel, None, [shape_of((-(-piece // 16) * 16 + PAD, model), BF)],
        lax.dynamic_slice_in_dim(w_out, here * piece, piece, 0), gain_attn.reshape(-1, LANES),
        gain_ffn.reshape(-1, LANES), head_bias, q_gain[None], k_gain[None], us=0.6,
    )[0]
    got_out = [own_out] + [pz(own_out, p) for p in range(1, fsdp)]

    x_chunk = step(
        halves_kernel, 0, [shape_of((chunk + 2 * PAD, model), BF)], own_in, Far(got_in), us=1.0
    )[0]
    xs = gather_first(x_chunk)

    xs = gather_second(xs)
    z_out, params = step(
        params_kernel, fsdp, [shape_of((fsdp * piece, model), BF), shape_of((8, model), F32)], Far(*got_out), us=0.6
    )
    out_same = gather_first(z_out)
    gu_blocks = -(-2 * ff // LANES)
    quarters = model // 2 // LANES
    padded = -(-ff_z // 16) * 16
    ff_piece = gu_blocks * half_z + quarters * padded
    own_ff = step(
        pack_kernel, (chips, fsdp, ff, ff_z), [shape_of((ff_piece, LANES), BF)],
        Far(w_gate), Far(w_up), Far(w_down), us=2.3,
    )[0]
    packed_ff = lax.all_gather(own_ff, ("fsdp", "core"), axis=0, tiled=True)


    n1, table, kinds, hots = step(
        norm_kernel, chips,
        [shape_of((span, model), BF), shape_of((span, LANES), F32)] + [shape_of((span, HEAD_DIM), BF)] * 2,
        joined(xs), jnp.asarray(turn_table(span)), params, scalars=seq_lengths, us=4.0, vmem=40,
    )
    out_same = gather_second(out_same)
    dy_chunk = step(halves_kernel, slots + PAD, [shape_of((chunk, model), BF)], own_in, Far(got_in), us=1.0)[0]
    dys = gather_first(dy_chunk)
    outs = step(
        attend_kernel, (chips, heads, fsdp),
        [Far(shape_of((span, width), BF))] * 3
        + [Far(shape_of((span, 2 * width), F32)), Far(shape_of((model, 3 * width), BF)), Far(shape_of((span, width), F32))]
        + [shape_of((chunk, width), BF)] * chips,
        Far(packed_qkv), n1, table, kinds, hots, params, us=FRONT_US, vmem=40,
    )
    q, k, v, pre, w_qkv, mix = outs[:6]
    mix_got = exchange(outs[6:])
    out_other = pc(stack(*[a for part in out_same for a in part], after=dys[1:]))
    w_o = step(
        w_out_kernel, (chips, fsdp, piece), [shape_of((model, model), BF)], joined(out_same), Far(out_other),
        us=1.5, scratch=[pltpu.VMEM((model, model), F32)],
    )[0]

    hidden_state, normed2 = step(
        functools.partial(mix_out_kernel, width), chips,
        [shape_of((chunk, model), F32), shape_of((chunk, model), BF)],
        Far(x_chunk), w_o, params, mix_got[0], *far(mix_got[1:]), us=2.2,
    )
    n2s = gather_first(normed2)
    dys = gather_second(dys)

    w_gu, w_d = step(
        unpack_kernel, (fsdp, ff, ff_z, ff_pad),
        [shape_of((model, 2 * ff_pad), BF), shape_of((ff_pad, model), BF)], Far(packed_ff), us=2.0,
    )

    def feed_forward(d):
        return step(
            ffn_kernel, (d, ff_pad),
            [shape_of((chunk, model), BF), shape_of((chunk, ff_pad), BF), shape_of((chunk, 2 * ff_pad), BF)],
            Far(*n2s[d]), Far(*dys[d]), w_gu, w_d, scalars=seq_lengths, us=3.3,
        )

    n2s_first, n2s = n2s, [[normed2]]
    ffn = [feed_forward(0)]
    n2s = gather_second(n2s_first)
    ffn += [feed_forward(d) for d in range(1, chips)]
    dn2_got = exchange([a[0] for a in ffn])

    packed_grad, gain2_part = step(
        ffn_grad_kernel, (chips, fsdp, ff, ff_z, ff_pad),
        [shape_of((2 * fsdp * ff_piece, LANES), BF), shape_of((8, model), F32)],
        joined(n2s), joined(dys), Far(*[a[1] for a in ffn]), Far(*[a[2] for a in ffn]), w_gu, params,
        scalars=seq_lengths, us=7.6, vmem=40,
    )
    ff_sum = lax.psum_scatter(packed_grad, ("fsdp", "core"), scatter_dimension=0, tiled=True)

    outs = step(
        functools.partial(hidden_back_kernel, width), chips,
        [shape_of((chunk, model), F32), shape_of((chunk, model), BF)] + [shape_of((chunk, width), BF)] * chips,
        hidden_state, Far(dy_chunk), params, w_o, dn2_got[0], *far(dn2_got[1:]), scalars=seq_lengths, us=2.2,
    )
    d_hidden, d_hidden_low = outs[:2]
    dmix_got = exchange(outs[2:])

    mine_o, theirs_o = step(
        out_grad_kernel, (chips, fsdp, width, piece), [shape_of((chips, fsdp, piece, model), BF)] * 2,
        d_hidden_low, *far(mix_got), us=2.2, scratch=[pltpu.VMEM((model, model), F32)],
    )
    got_o = pc(theirs_o)

    layout, rows = scatter_layout(fsdp * piece, 2)
    by_chip = step(
        core_sum_kernel, layout, [shape_of((n, model), BF) for n in rows], mine_o, Far(got_o), us=1.0
    )
    chip_o = scatter_first(by_chip, 2)
    layout, rows = scatter_layout(chunk, 1)
    downs = step(
        down_kernel, layout, [shape_of((n, model), BF) for n in rows], w_d, *[a[1] for a in ffn], us=1.8
    )
    down_got = scatter_first(downs, 1)

    d_qkv, small_part = step(
        attend_back_kernel, (chips, heads, width),
        [shape_of((span, 3 * width), BF), shape_of((8, LANES), F32)],
        Far(*dmix_got), *far((table, q, k, v, mix, pre)), params, us=BACK_US, vmem=40,
        scratch=[pltpu.VMEM((span, HEAD_DIM), BF)] * 2 + [pltpu.VMEM((span, width), F32)] * 3,
    )

    mine, theirs, gain1_part = step(
        qkv_grad_kernel, fsdp, [shape_of((fsdp * half_z, 3 * width), BF)] * 2 + [shape_of((8, model), F32)],
        Far(n1), d_qkv, Far(w_qkv), params, us=3.0, scratch=[pltpu.VMEM((model, 3 * width), F32)],
    )
    got = pc(theirs)
    chip_o = scatter_second(chip_o, 2)

    d_n1 = step(project_back_kernel, None, [shape_of((chunk, model), BF)] * chips, d_qkv, Far(w_qkv), us=2.0)
    dn1_got = exchange(d_n1)

    down_got = scatter_second(down_got, 1)
    count = body + PAD + model // LANES * piece
    messages = step(
        message_kernel, (fsdp, len(chip_o)), [shape_of((count, LANES), BF)] * fsdp,
        mine, Far(got), gain1_part, gain2_part, small_part, *far(chip_o), us=1.5,
    )
    z_got = [messages[0]] + [pz(messages[p], p) for p in range(1, fsdp)]

    ff_all = lax.all_gather(stack(ff_sum), ("chip", "core"), axis=0, tiled=True)
    own_result, their_result = step(
        output_kernel, len(down_got), [shape_of((slots, model), BF)] * 2,
        Far(hidden_state), *far(down_got), scalars=seq_lengths, us=1.8,
    )
    got_result = pc(their_result)
    z_sum = step(sum_kernel, None, [shape_of((count, LANES), BF)], z_got[0], *far(z_got[1:]), us=1.0)[0]
    same = gather_first(z_sum)

    own_grad, their_grad = step(
        input_back_kernel, chips, [shape_of((slots, model), F32), shape_of((slots, model), BF)],
        Far(x_chunk), Far(d_hidden), params, dn1_got[0], *far(dn1_got[1:]), us=1.8,
    )
    got_grad = pc(their_grad)
    same = gather_second(same)
    other = pc(stack(*[a for part in same for a in part]))
    grad_gate, grad_up, grad_down = step(
        ffn_final_kernel, (chips, fsdp, ff, ff_z),
        [shape_of((rows_z, hidden), F32)] * 2 + [shape_of((hidden // fsdp, model), F32)], Far(ff_all), us=5.0,
    )
    grad_query, grad_key, grad_value, grad_out, small_sum = step(
        projections_final_kernel, (chips, width, half_z, piece),
        [shape_of((rows_z, model), F32)] * 4 + [shape_of((PAD, LANES), F32)], joined(same), Far(other), us=3.0,
    )
    output, grad_inputs = step(
        by_sequence_kernel, None, [shape_of((2, slots, model), BF), shape_of((2, slots, model), F32)],
        own_result, Far(got_result), own_grad, Far(got_grad), us=1.0,
    )
    per = rows_z // LANES
    grad_bias = lax.dynamic_slice(small_sum, (SAME_ROW, depth * heads_z), (2, heads_z)).T
    grad_q_gain = lax.dynamic_slice(small_sum, (Q_ROW, depth * dims_z), (1, dims_z))[0]
    grad_k_gain = lax.dynamic_slice(small_sum, (K_ROW, depth * dims_z), (1, dims_z))[0]
    return (
        output, grad_inputs, grad_query, grad_key, grad_value, grad_out, grad_gate, grad_up, grad_down,
        small_sum[:per].reshape(-1), small_sum[2 : 2 + per].reshape(-1), grad_bias, grad_q_gain, grad_k_gain,
    )


def solution(mesh):
    ctx, fsdp = mesh.shape["ctx"], mesh.shape["fsdp"]
    chips = ctx // 2
    split = Mesh(mesh.devices.reshape(chips, 2, fsdp), ("chip", "core", "fsdp"))
    rows, row = P("fsdp", None), P("fsdp")
    block, ids = P("fsdp", ("chip", "core"), None), P("fsdp", ("chip", "core"))
    return jax.shard_map(
        functools.partial(layer, chips, fsdp),
        mesh=split,
        in_specs=(block, ids, ids, row) + (rows,) * 7 + (row, row, rows, row, row, block),
        out_specs=(block, block) + (rows,) * 7 + (row, row, rows, row, row),
        check_vma=False,
    )
```

```python
import functools

import jax
import jax.numpy as jnp
import ml_dtypes
import numpy as np
from jax import lax
from jax.experimental import pallas as pl
from jax.experimental.pallas import tpu as pltpu
from jax.sharding import Mesh
from jax.sharding import PartitionSpec as P

EPSILON = 1e-05
ROPE_BASE = 10000.0
NEG_FILL = -1e30
HEAD_DIM = 64
HALF = HEAD_DIM // 2
BF = jnp.bfloat16
F32 = jnp.float32
PAD = 16
LANES = 128
FRONT_US, BACK_US = 30.0, 20.0
PEAK = 3.45e9

NT = (((1,), (1,)), ((), ()))
TN = (((0,), (0,)), ((), ()))
NN = (((1,), (0,)), ((), ()))

Q_ROW, K_ROW, SAME_ROW, OTHER_ROW = 4, 5, 6, 7


def mm(left, right, dims=NN):
    return lax.dot_general(left, right, dims, preferred_element_type=F32)


class Far:
    def __init__(self, *arrays):
        self.arrays = arrays


def kernel_call(kernel, out_shapes, *operands, scalars=None, scratch=(), us=1.0, vmem=40, after=()):
    vmem_spec, any_spec = pl.BlockSpec(memory_space=pltpu.VMEM), pl.BlockSpec(memory_space=pl.ANY)
    arrays, specs, fetched, sources = [], [], [], []
    for operand in operands:
        if isinstance(operand, Far):
            sources.append((len(arrays), len(operand.arrays)))
            arrays += operand.arrays
            specs += [any_spec] * len(operand.arrays)
            first = operand.arrays[0]
            rows = sum(a.shape[0] for a in operand.arrays)
            fetched.append(pltpu.VMEM((rows,) + first.shape[1:], first.dtype))
        else:
            sources.append((len(arrays), 0))
            arrays.append(operand)
            specs.append(vmem_spec)
    far_out = [isinstance(a, Far) for a in out_shapes]
    out_shapes = [a.arrays[0] if isinstance(a, Far) else a for a in out_shapes]
    shipped = [pltpu.VMEM(a.shape, a.dtype) for a, far in zip(out_shapes, far_out) if far]
    n_arrays, n_out, n_own, n_fetched = len(arrays), len(out_shapes), len(scratch), len(fetched)
    n_sems = sum(count for _, count in sources) + len(shipped)
    sems = [pltpu.SemaphoreType.DMA((n_sems,))] if n_sems else []
    head_specs = [] if scalars is None else [pl.BlockSpec(memory_space=pltpu.SMEM)]
    head_arrays = [] if scalars is None else [scalars]
    n_head = len(head_arrays)

    def whole(*refs):
        head, refs = refs[:n_head], refs[n_head:]
        given, refs = refs[:n_arrays], refs[n_arrays + len(after) :]
        outs, refs = list(refs[:n_out]), refs[n_out:]
        own, refs = refs[:n_own], refs[n_own:]
        local, refs = refs[:n_fetched], refs[n_fetched:]
        sem, at, copies, ins = (refs[-1] if n_sems else None), 0, [], []
        for first, count in sources:
            if not count:
                ins.append(given[first])
                continue
            target, local = local[0], local[1:]
            row = 0
            for ref in given[first : first + count]:
                part = target if count == 1 else target.at[pl.ds(row, ref.shape[0])]
                row += ref.shape[0]
                copies.append(pltpu.make_async_copy(ref, part, sem.at[at]))
                copies[-1].start()
                at += 1
            ins.append(target)
        ship, waits = [], []
        for n in range(n_out):
            if far_out[n]:

                def start(source=refs[len(ship)], target=outs[n], at=at + len(ship), started=[]):
                    if not started:
                        started.append(pltpu.make_async_copy(source, target, sem.at[at]))
                        started[0].start()
                        waits.append(started[0])

                outs[n] = refs[len(ship)]
                ship.append(start)
        for copy in copies:
            copy.wait()
        extra = {"ship": ship} if ship else {}
        outs[-1][...] = jnp.zeros(outs[-1].shape, F32)
        kernel(*head, *ins, *outs[:-1], *own, **extra)
        for start in ship:
            start()
        for copy in waits:
            copy.wait()

    return pl.pallas_call(
        whole,
        out_shape=out_shapes,
        in_specs=head_specs + specs + [any_spec] * len(after),
        out_specs=[any_spec if far else vmem_spec for far in far_out],
        scratch_shapes=list(scratch) + fetched + shipped + sems,
        cost_estimate=pl.CostEstimate(flops=int(us * PEAK), bytes_accessed=0, transcendentals=0),
        compiler_params=pltpu.CompilerParams(vmem_limit_bytes=vmem * 2**20),
    )(*head_arrays, *arrays, *after)


def shape_of(dims, dtype):
    return jax.ShapeDtypeStruct(tuple(dims), dtype)


def place():
    return lax.axis_index("core"), lax.axis_index("chip"), lax.axis_index("fsdp")


def stack_kernel(counts, *refs):
    at = 0
    for ref, count in zip(refs[:-1], counts):
        refs[-1][pl.ds(at, count), :] = ref[pl.ds(0, count), :]
        at += count


def lane_of(shape):
    return lax.broadcasted_iota(jnp.int32, shape, 1)


def head_sum(values):
    row = lax.broadcasted_iota(jnp.int32, (LANES, LANES), 0) // HEAD_DIM
    col = lax.broadcasted_iota(jnp.int32, (LANES, LANES), 1) // HEAD_DIM
    ones = (row == col).astype(BF)
    high = values.astype(BF)
    low = (values - high.astype(F32)).astype(BF)
    return mm(high, ones) + mm(low, ones)


def row_totals(values):
    ones = jnp.ones((8, values.shape[1]), BF)
    high = values.astype(BF)
    low = (values - high.astype(F32)).astype(BF)
    return (mm(ones, high, NT) + mm(ones, low, NT))[:1]


def half_swap(values):
    first = lane_of(values.shape) % HEAD_DIM < HALF
    return jnp.where(first, pltpu.roll(values, LANES - HALF, 1), pltpu.roll(values, HALF, 1))


def rotary(table):
    lane = lane_of(table.shape)
    base = jnp.where(lane < HEAD_DIM, table, pltpu.roll(table, HEAD_DIM, 1))
    other = half_swap(base)
    first = lane % HEAD_DIM < HALF
    return jnp.where(first, base, other), jnp.where(first, -other, base)


def one_lane(row, index):
    return jnp.sum(jnp.where(lane_of(row.shape) == index, row, 0.0), axis=1, keepdims=True)


def key_features(kind, params, head):
    same = one_lane(params[SAME_ROW : SAME_ROW + 1, :LANES], head)
    other = one_lane(params[OTHER_ROW : OTHER_ROW + 1, :LANES], head)
    return jnp.where(kind == 0.0, other, jnp.where(kind == 1.0, same, NEG_FILL)).astype(BF)


def scale_of(x):
    return lax.rsqrt(jnp.mean(x * x, axis=-1, keepdims=True) + EPSILON)


def norm_back(grad, x, gain):
    scale = scale_of(x)
    unit = x * scale
    scaled = grad * gain
    return scale * (scaled - unit * jnp.mean(scaled * unit, axis=-1, keepdims=True))


def input_kernel(inputs, times, variates, cotangent, own, other):
    slots = inputs.shape[1]
    core = lax.axis_index("core")
    for index, out in ((core, own), (1 - core, other)):
        out[pl.ds(0, slots), :] = inputs[index]
        time, variate = times[pl.ds(index, 1), :], variates[pl.ds(index, 1), :]
        rows = [time >> 8, time & 255, variate, jnp.zeros((PAD - 3, slots), jnp.int32)]
        out[pl.ds(slots, PAD), :] = jnp.zeros((PAD, out.shape[1]), BF)
        out[pl.ds(slots, PAD), pl.ds(0, slots)] = jnp.concatenate(rows, 0).astype(F32).astype(BF)
        out[pl.ds(slots + PAD, slots), :] = cotangent[index]


def halves_kernel(at, own, other, out):
    count = out.shape[0] // 2
    out[pl.ds(0, count), :] = own[pl.ds(at, count), :]
    out[pl.ds(count, count), :] = other[pl.ds(at, count), :]


def cut_kernel(side, up, first, second):
    cut = first.shape[0]
    first[...] = side[pl.ds(0, cut), :]
    second[...] = up[pl.ds(cut, second.shape[0]), :]


def weight_kernel(width, w_query, w_key, w_value, out):
    core, chip, _ = place()
    half = w_query.shape[0] // 2
    at = 0
    for ref in (w_query, w_key, w_value):
        for n in range(width // LANES):
            col = pl.multiple_of(chip * width + n * LANES, LANES)
            row = pl.multiple_of(core * half, 16)
            out[pl.ds(at, half), :] = ref[pl.ds(row, half), pl.ds(col, LANES)]
            at += half


def small_kernel(gain_attn, gain_ffn, head_bias, q_gain, k_gain, out):
    depth = lax.axis_index("fsdp")
    lane = lane_of((1, LANES))
    rows = [gain_attn[...].astype(F32), gain_ffn[...].astype(F32)]
    rows = [jnp.concatenate([r, jnp.zeros((2 - r.shape[0], LANES), F32)], 0) if r.shape[0] < 2 else r for r in rows]
    for ref in (q_gain, k_gain):
        value, dims = ref[...].astype(F32), ref.shape[1]
        row = jnp.zeros((1, LANES), F32)
        for j in range(dims):
            row = jnp.where(lane % HEAD_DIM == depth * dims + j, value[:, j : j + 1], row)
        rows.append(row)
    value, heads = head_bias[...].astype(F32), head_bias.shape[0]
    for n in range(2):
        row = jnp.zeros((1, LANES), F32)
        for j in range(heads):
            row = jnp.where(lane == depth * heads + j, value[j : j + 1, n : n + 1], row)
        rows.append(row)
    rows.append(jnp.zeros((PAD - 8, LANES), F32))
    out[...] = jnp.concatenate(rows, 0).astype(BF)


def layers_kernel(*refs):
    piece = refs[0].shape[0]
    for p, ref in enumerate(refs[:-1]):
        refs[-1][pl.ds(p * piece, piece), :] = ref[...]


def params_kernel(depths, pieces, params):
    depth = lax.axis_index("fsdp")
    rows_z = params.shape[1] // depths
    params[...] = jnp.zeros_like(params)
    total = None
    for p in range(depths):
        small = pieces[pl.ds(p * PAD, PAD), :].astype(F32)
        total = small if total is None else total + small
        for n in range(rows_z // LANES):
            col = pl.multiple_of((depth ^ p) * rows_z + n * LANES, LANES)
            params[pl.ds(0, 1), pl.ds(col, LANES)] = small[n : n + 1]
            params[pl.ds(1, 1), pl.ds(col, LANES)] = small[2 + n : 3 + n]
    for n in (Q_ROW, K_ROW, SAME_ROW, OTHER_ROW):
        params[pl.ds(n, 1), pl.ds(0, LANES)] = total[n : n + 1]


def turn_table(span):
    coarse = -(-span // 16)
    frequency = ROPE_BASE ** (-np.arange(HALF) * (2.0 / HEAD_DIM))
    steps = np.concatenate([16.0 * np.arange(coarse), np.arange(16.0)])
    angles = steps[:, None] * frequency
    exact = np.concatenate([np.cos(angles), np.sin(angles)], axis=1).astype(np.float32)
    parts, rest = [], exact
    for _ in range(3):
        low = rest.astype(ml_dtypes.bfloat16)
        parts.append(low)
        rest = rest - low.astype(np.float32)
    return np.concatenate(parts, axis=1)


def slot_table(lengths, ids, turns, slots, d):
    tables = []
    coarse = turns.shape[0] - 16
    for c in range(2):
        rows = ids[c][:, :slots].astype(F32)
        high, low, variate = rows[0:1].astype(jnp.int32), rows[1:2].astype(jnp.int32), rows[2:3].astype(jnp.int32)
        time = high * 256 + low
        index = lax.broadcasted_iota(jnp.int32, (coarse, slots), 0)
        hot_a = jnp.where(index == time >> 4, 1.0, 0.0).astype(BF)
        index = lax.broadcasted_iota(jnp.int32, (16, slots), 0)
        hot_b = jnp.where(index == (time & 15), 1.0, 0.0).astype(BF)
        turn_a, turn_b = mm(hot_a, turns[:coarse], TN), mm(hot_b, turns[coarse:], TN)
        turn_a = turn_a[:, :64] + turn_a[:, 64:128] + turn_a[:, 128:]
        turn_b = turn_b[:, :64] + turn_b[:, 64:128] + turn_b[:, 128:]
        cos_a, sin_a, cos_b, sin_b = turn_a[:, :HALF], turn_a[:, HALF:], turn_b[:, :HALF], turn_b[:, HALF:]
        index = lax.broadcasted_iota(jnp.int32, (HEAD_DIM, slots), 0)
        hot = jnp.where(index == variate, 1.0, 0.0).astype(BF)
        eye = lax.broadcasted_iota(jnp.int32, (HEAD_DIM, HEAD_DIM), 0) == lane_of((HEAD_DIM, HEAD_DIM))
        kind = mm(hot, jnp.where(eye, 1.0, 0.0).astype(BF), TN)
        tables.append(jnp.concatenate([cos_a * cos_b - sin_a * sin_b, sin_a * cos_b + cos_a * sin_b, kind], axis=1))
    table = jnp.concatenate(tables, axis=0)
    hidden = jnp.logical_and(lane_of(table.shape) >= HEAD_DIM, jnp.logical_not(valid_rows(lengths, 2, slots, d)))
    return jnp.where(hidden, 2.0, table)


def norm_kernel(chips, lengths, xs, turns, params, n1, tables, kinds, hots):
    chunk = n1.shape[0] // chips
    slots = chunk // 2
    for d in range(chips):
        rows = pl.ds(d * chunk, chunk)
        x = xs[pl.ds(d * (chunk + 2 * PAD), chunk + 2 * PAD), :]
        ids = [x[slots : slots + PAD], x[2 * slots + PAD :]]
        table = slot_table(lengths, ids, turns[...], slots, d)
        tables[rows, :] = table
        kind = table[:, HEAD_DIM:]
        kinds[rows, :] = kind.astype(BF)
        hots[rows, :] = (kind == 1.0).astype(BF)
        x = jnp.concatenate([x[:slots], x[slots + PAD : 2 * slots + PAD]], axis=0).astype(F32)
        n1[rows, :] = (x * scale_of(x) * params[pl.ds(0, 1), :]).astype(BF)


def attend_kernel(cfg, packed, n1, tables, kinds, hots, params, *refs, ship):
    chips, heads, depths = cfg
    q, k, v, pre, w, mix = refs[:6]
    lows = refs[6:]
    span, width = q.shape
    chunk = span // chips
    half = n1.shape[1] // depths // 2
    blocks = w.shape[1] // LANES
    for b in range(2 * depths):
        for n in range(blocks):
            w[pl.ds(b * half, half), pl.ds(n * LANES, LANES)] = packed[pl.ds((b * blocks + n) * half, half), :]
    ship[4]()
    for d in range(chips):
        rows = pl.ds(d * chunk, chunk)
        cosine, sine = rotary(tables[rows, :])
        both = mm(n1[rows, :], w[...])
        v[rows, :] = both[:, 2 * width :].astype(BF)
        pre[rows, :] = both[:, : 2 * width]
        for source, row, target in ((0, Q_ROW, q), (width, K_ROW, k)):
            gain = params[pl.ds(row, 1), pl.ds(0, LANES)]
            for g in range(width // LANES):
                value = both[:, source + LANES * g : source + LANES * (g + 1)]
                scale = lax.rsqrt(head_sum(value * value) * (1.0 / HEAD_DIM) + EPSILON)
                normed = value * scale * gain
                target[rows, pl.ds(LANES * g, LANES)] = (normed * cosine + half_swap(normed) * sine).astype(BF)
    for n in range(4):
        ship[n]()
    for h in range(heads):
        lanes = pl.ds(HEAD_DIM * h, HEAD_DIM)
        features = key_features(kinds[...].astype(F32), params, lax.axis_index("chip") * heads + h)
        keys = jnp.concatenate([k[:, lanes], features], axis=1)
        values = v[:, lanes]
        for d in range(chips):
            rows = pl.ds(d * chunk, chunk)
            query = jnp.concatenate([q[rows, lanes] * BF(0.125), hots[rows, :]], axis=1)
            terms = jnp.exp(mm(query, keys, NT))
            denom = jnp.sum(terms, axis=-1, keepdims=True)
            part = mm(terms.astype(BF), values) / denom
            mix[rows, lanes] = part
            lows[d][:, lanes] = part.astype(BF)


def mix_out_kernel(width, chips, own, w_out, params, *refs):
    pieces, (h_ref, n2) = refs[:chips], refs[chips:]
    chunk = h_ref.shape[0]
    slots = chunk // 2
    total = None
    for d in range(chips):
        row = pl.multiple_of((lax.axis_index("chip") ^ d) * width, LANES)
        term = mm(pieces[d][...], w_out[pl.ds(row, width), :])
        total = term if total is None else total + term
    x = jnp.concatenate([own[pl.ds(0, slots), :], own[pl.ds(slots + PAD, slots), :]], axis=0)
    h = x.astype(F32) + total
    h_ref[...] = h
    n2[...] = (h * scale_of(h) * params[pl.ds(1, 1), :]).astype(BF)


def valid_rows(lengths, halves, slots, d):
    core, chip, _ = place()
    row = lax.broadcasted_iota(jnp.int32, (slots, 1), 0)
    here = 2 * chip + core
    return jnp.concatenate([(here ^ (2 * d + c)) * slots + row < lengths[core] for c in range(halves)], axis=0)


def pack_kernel(cfg, w_gate, w_up, w_down, packed):
    chips, depths, ff, ff_z = cfg
    half, hidden = w_gate.shape[0] // 2, w_gate.shape[1]
    model = w_down.shape[1]
    blocks = -(-2 * ff // LANES)
    padded = -(-ff_z // 16) * 16
    quarters = model // 2 // LANES
    core, chip, _ = place()
    rows = pl.ds(pl.multiple_of(core * half, 16), half)
    for t in range(chips):

        @pl.when(chip == t)
        def _():
            parts = []
            for ref in (w_gate, w_up):
                both = ref[rows, :]
                parts += [both[:, n * (hidden // depths) + t * ff_z :][:, :ff_z] for n in range(depths)]
            if 2 * ff % LANES:
                parts.append(jnp.zeros((half, blocks * LANES - 2 * ff), BF))
            tight = jnp.concatenate(parts, axis=1)
            for n in range(blocks):
                packed[pl.ds(n * half, half), :] = tight[:, n * LANES : (n + 1) * LANES]
            for n in range(quarters):
                col = pl.multiple_of(core * (model // 2) + n * LANES, LANES)
                value = w_down[pl.ds(t * ff_z, ff_z), pl.ds(col, LANES)]
                if padded > ff_z:
                    value = jnp.concatenate([value, jnp.zeros((padded - ff_z, LANES), BF)], axis=0)
                packed[pl.ds(blocks * half + n * padded, padded), :] = value


def unpack_kernel(cfg, packed, w_gu, w_d):
    depths, ff, ff_z, ff_pad = cfg
    model = w_gu.shape[0]
    half = model // depths // 2
    blocks = -(-2 * ff // LANES)
    padded = -(-ff_z // 16) * 16
    quarters = model // 2 // LANES
    piece = blocks * half + quarters * padded
    w_gu[...] = jnp.zeros_like(w_gu)
    w_d[...] = jnp.zeros_like(w_d)
    for z in range(depths):
        for c in range(2):
            base = (2 * z + c) * piece
            rows = pl.ds((2 * z + c) * half, half)
            both = jnp.concatenate([packed[pl.ds(base + n * half, half), :] for n in range(blocks)], axis=1)
            w_gu[rows, pl.ds(0, ff)] = both[:, :ff]
            w_gu[rows, pl.ds(ff_pad, ff)] = both[:, ff : 2 * ff]
            for n in range(quarters):
                at = base + blocks * half + n * padded
                w_d[pl.ds(z * ff_z, ff_z), pl.ds(c * model // 2 + n * LANES, LANES)] = packed[pl.ds(at, ff_z), :]


def ffn_kernel(cfg, lengths, n2, dy, w_gu, w_d, dn2, act, dgu):
    d, ff_pad = cfg
    n2 = n2[...]
    dy = jnp.where(valid_rows(lengths, 2, n2.shape[0] // 2, d), dy[...], jnp.zeros_like(n2))
    pre = mm(n2, w_gu[...])
    gate, up = pre[:, :ff_pad], pre[:, ff_pad:]
    sig = jax.nn.sigmoid(gate)
    silu = gate * sig
    low = (silu * up).astype(BF)
    act[...] = low
    d_act = mm(dy, w_d[...], NT)
    d_up = (d_act * silu).astype(BF)
    d_gate = (d_act * up * sig * (1.0 + gate * (1.0 - sig))).astype(BF)
    both = jnp.concatenate([d_gate, d_up], axis=1)
    dgu[...] = both
    dn2[...] = mm(both, w_gu[...], NT).astype(BF)


def down_kernel(places, w_d, *refs):
    acts, outs = refs[: len(places)], refs[len(places) :]
    for act, (n, row) in zip(acts, places):
        outs[n][pl.ds(row, act.shape[0]), :] = mm(act[...], w_d[...]).astype(BF)


def core_sum_kernel(places, mine, got, *outs):
    depths, piece = mine.shape[1:3]
    for d, (n, row) in enumerate(places):
        for p in range(depths):
            total = mine[d, p].astype(F32) + got[d, p].astype(F32)
            outs[n][pl.ds(row + p * piece, piece), :] = total.astype(BF)


def half_sum_kernel(keep, got, own, send):
    rows = own.shape[0]
    total = (keep[...].astype(F32) + got[...].astype(F32)).astype(BF)
    own[...] = total[:rows]
    send[...] = total[rows:]


def ffn_grad_kernel(cfg, lengths, n2, dy, act, dgu, w_gu, params, packed, gain2):
    chips, depths, ff, ff_z, ff_pad = cfg
    model = w_gu.shape[0]
    chunk = n2.shape[0] // chips
    for d in range(chips):
        rows = pl.ds(d * chunk, chunk)
        part = dy[rows, :]
        dy[rows, :] = jnp.where(valid_rows(lengths, 2, chunk // 2, d), part, jnp.zeros_like(part))
    half = model // depths // 2
    blocks = -(-2 * ff // LANES)
    padded = -(-ff_z // 16) * 16
    quarters = model // 2 // LANES
    piece = blocks * half + quarters * padded
    for b in range(2 * depths):
        rows = pl.ds(b * half, half)
        grad = mm(n2[:, rows], dgu[...], TN)
        gain = params[pl.ds(1, 1), rows]
        gain2[pl.ds(0, 1), rows] = row_totals(grad * w_gu[rows, :].astype(F32)) / gain
        tight = jnp.concatenate([grad[:, :ff], grad[:, ff_pad : ff_pad + ff]], axis=1).astype(BF)
        if 2 * ff % LANES:
            tight = jnp.concatenate([tight, jnp.zeros((half, blocks * LANES - 2 * ff), BF)], axis=1)
        for n in range(blocks):
            packed[pl.ds(b * piece + n * half, half), :] = tight[:, n * LANES : (n + 1) * LANES]
    for z in range(depths):
        grad = mm(act[:, pl.ds(z * ff_z, ff_z)], dy[...], TN).astype(BF)
        if padded > ff_z:
            grad = jnp.concatenate([grad, jnp.zeros((padded - ff_z, model), BF)], axis=0)
        for c in range(2):
            for n in range(quarters):
                at = (2 * z + c) * piece + blocks * half + n * padded
                col = c * model // 2 + n * LANES
                packed[pl.ds(at, padded), :] = grad[:, col : col + LANES]


def ffn_final_kernel(cfg, packed, g_gate, g_up, g_down):
    chips, depths, ff, ff_z = cfg
    model = g_down.shape[1]
    half = model // depths // 2
    hidden_z = chips * ff_z
    blocks = -(-2 * ff // LANES)
    padded = -(-ff_z // 16) * 16
    quarters = model // 2 // LANES
    piece = blocks * half + quarters * padded
    for t in range(chips):
        for c in range(2):
            base = (2 * t + c) * piece
            both = jnp.concatenate([packed[pl.ds(base + n * half, half), :] for n in range(blocks)], axis=1).astype(F32)
            for z in range(depths):
                cols = pl.ds(z * hidden_z + t * ff_z, ff_z)
                g_gate[pl.ds(c * half, half), cols] = both[:, z * ff_z : (z + 1) * ff_z]
                g_up[pl.ds(c * half, half), cols] = both[:, ff + z * ff_z : ff + (z + 1) * ff_z]
            for n in range(quarters):
                at = base + blocks * half + n * padded
                rows = pl.ds(t * ff_z, ff_z)
                g_down[rows, pl.ds(c * model // 2 + n * LANES, LANES)] = packed[pl.ds(at, ff_z), :].astype(F32)


def output_kernel(count, lengths, h, *refs):
    terms, (out, low) = refs[:count], refs[count:]
    slots = out.shape[0]
    total = h[...]
    for ref in terms:
        total = total + ref[...].astype(F32)
    total = jnp.where(valid_rows(lengths, 2, slots, 0), total, 0.0).astype(BF)
    out[...] = total[:slots]
    low[...] = total[slots:]


def hidden_back_kernel(width, chips, lengths, h, dy, params, w_out, *refs):
    terms, (d_h, d_low), d_mix = refs[:chips], refs[chips : chips + 2], refs[chips + 2 :]
    grad = terms[0][...].astype(F32)
    for ref in terms[1:]:
        grad = grad + ref[...].astype(F32)
    own = jnp.where(valid_rows(lengths, 2, dy.shape[0] // 2, 0), dy[...].astype(F32), 0.0)
    total = own + norm_back(grad, h[...], params[pl.ds(1, 1), :])
    d_h[...] = total
    low = total.astype(BF)
    d_low[...] = low
    for d in range(chips):
        row = pl.multiple_of((lax.axis_index("chip") ^ d) * width, LANES)
        d_mix[d][...] = mm(low, w_out[pl.ds(row, width), :], NT).astype(BF)


def out_grad_kernel(cfg, d_low, *refs):
    chips, depths, width, piece = cfg
    mixes, (mine, theirs, full) = refs[:chips], refs[chips:]
    core, chip, depth = place()
    rows_z = full.shape[0] // depths
    for d in range(chips):
        row = pl.multiple_of((chip ^ d) * width, LANES)
        full[pl.ds(row, width), :] = mm(mixes[d][...], d_low[...], TN)
    for out, c in ((mine, core), (theirs, 1 - core)):
        for d in range(chips):
            for p in range(depths):
                row = (depth ^ p) * rows_z + c * (rows_z // 2) + (chip ^ d) * piece
                out[d, p] = full[pl.ds(pl.multiple_of(row, 8), piece), :].astype(BF)


def sum_kernel(*refs):
    total = refs[0][...].astype(F32)
    for ref in refs[1:-1]:
        total = total + ref[...].astype(F32)
    refs[-1][...] = total.astype(BF)


def input_back_kernel(chips, own_x, d_h, params, *refs):
    terms, (out, low) = refs[:chips], refs[chips:]
    slots = out.shape[0]
    grad = terms[0][...].astype(F32)
    for ref in terms[1:]:
        grad = grad + ref[...].astype(F32)
    x = jnp.concatenate([own_x[pl.ds(0, slots), :], own_x[pl.ds(slots + PAD, slots), :]], axis=0).astype(F32)
    total = d_h[...] + norm_back(grad, x, params[pl.ds(0, 1), :])
    out[...] = total[:slots]
    low[...] = total[slots:].astype(BF)


def by_sequence_kernel(result, their_result, grad_x, their_grad, out, grad):
    core = lax.axis_index("core")
    out[core] = result[...]
    out[1 - core] = their_result[...]
    grad[core] = grad_x[...]
    grad[1 - core] = their_grad[...].astype(F32)


def attend_back_kernel(cfg, *refs):
    chips, heads, width = cfg
    dmix, tables, q, k, v, mix, pre, params, d_qkv, smalls = refs[:10]
    kinds, hots, dq_scr, dk_scr, dv_scr = refs[10:]
    span = k.shape[0]
    chunk = span // chips
    dk_scr[...] = jnp.zeros_like(dk_scr)
    dv_scr[...] = jnp.zeros_like(dv_scr)
    smalls[...] = jnp.zeros_like(smalls)
    for d in range(chips):
        rows = pl.ds(d * chunk, chunk)
        kind = tables[rows, HEAD_DIM:]
        kinds[rows, :] = kind.astype(BF)
        hots[rows, :] = (kind == 1.0).astype(BF)
    lane = lane_of((1, LANES))

    def step(c, carry):
        part = pl.ds(pl.multiple_of(c * chunk, chunk), chunk)
        query_hot = hots[part, :]
        for h in range(heads):
            lanes = pl.ds(HEAD_DIM * h, HEAD_DIM)
            key = k[:, lanes]
            index = lax.axis_index("chip") * heads + h
            keys = jnp.concatenate([key, key_features(kinds[...].astype(F32), params, index)], axis=1)
            query = q[part, lanes] * BF(0.125)
            grad = dmix[part, lanes]
            product = mix[part, lanes] * grad.astype(F32)
            high = product.astype(BF)
            low = (product - high.astype(F32)).astype(BF)
            ones = jnp.ones((8, HEAD_DIM), BF)
            delta = (mm(ones, high, NT) + mm(ones, low, NT))[:1]
            terms = jnp.exp(mm(keys, jnp.concatenate([query, query_hot], axis=1), NT))
            prob = terms * (1.0 / jnp.sum(terms, axis=0, keepdims=True))
            d_score = (prob * (mm(v[:, lanes], grad, NT) - delta)).astype(BF)
            dk_scr[:, lanes] += mm(d_score, query)
            dv_scr[:, lanes] += mm(prob.astype(BF), grad)
            both = mm(d_score, jnp.concatenate([key, hots[...]], axis=1), TN)
            dq_scr[part, lanes] = both[:, :HEAD_DIM] * 0.125
            pairs = both[:, HEAD_DIM:]
            hot = query_hot.astype(F32)
            for row, weight in ((SAME_ROW, hot), (OTHER_ROW, 1.0 - hot)):
                value = jnp.sum(jnp.sum(pairs * weight, axis=0, keepdims=True), axis=1, keepdims=True)
                smalls[pl.ds(row, 1), :] += jnp.where(lane == index, value, 0.0)
        return carry

    lax.fori_loop(0, chips, step, 0)
    for d in range(chips):
        part = pl.ds(d * chunk, chunk)
        cosine, sine = rotary(tables[part, :])
        for n, (grads, row) in enumerate(((dq_scr, Q_ROW), (dk_scr, K_ROW))):
            gain = params[pl.ds(row, 1), pl.ds(0, LANES)]
            for g in range(width // LANES):
                grad = grads[part, pl.ds(LANES * g, LANES)]
                value = pre[part, pl.ds(n * width + LANES * g, LANES)]
                scale = lax.rsqrt(head_sum(value * value) * (1.0 / HEAD_DIM) + EPSILON)
                unit = value * scale
                d_normed = grad * cosine - half_swap(grad) * sine
                total = jnp.sum(d_normed * unit, axis=0, keepdims=True)
                smalls[pl.ds(row, 1), :] += total + pltpu.roll(total, HEAD_DIM, 1)
                scaled = d_normed * gain
                mean = head_sum(scaled * unit) * (1.0 / HEAD_DIM)
                d_qkv[part, pl.ds(n * width + LANES * g, LANES)] = (scale * (scaled - unit * mean)).astype(BF)
        d_qkv[part, pl.ds(2 * width, width)] = dv_scr[part, :].astype(BF)


def qkv_grad_kernel(depths, n1, d_qkv, w, params, mine, theirs, gain1, full):
    core, _, depth = place()
    model = n1.shape[1]
    half = model // depths // 2
    tile = 256
    for n in range(model // tile):
        rows = pl.ds(n * tile, tile)
        grad = mm(n1[:, rows], d_qkv[...], TN)
        full[rows, :] = grad
        gain1[pl.ds(0, 1), rows] = row_totals(grad * w[rows, :].astype(F32)) / params[pl.ds(0, 1), rows]
    for out, c in ((mine, core), (theirs, 1 - core)):
        for p in range(depths):
            row = pl.multiple_of((2 * (depth ^ p) + c) * half, 16)
            out[pl.ds(p * half, half), :] = full[pl.ds(row, half), :].astype(BF)


def project_back_kernel(d_qkv, w, *outs):
    chunk = outs[0].shape[0]
    for n, out in enumerate(outs):
        out[...] = mm(d_qkv[pl.ds(n * chunk, chunk), :], w[...], NT).astype(BF)


def message_kernel(cfg, mine, got, gain1, gain2, small, *refs):
    depths, count = cfg
    parts, outs = refs[:count], refs[count:]
    half = mine.shape[0] // depths
    blocks = mine.shape[1] // LANES
    per = 2 * half // LANES
    for p, out in enumerate(outs):
        rows = pl.ds(p * half, half)
        both = (mine[rows, :].astype(F32) + got[rows, :].astype(F32)).astype(BF)
        for n in range(blocks):
            out[pl.ds(n * half, half), :] = both[:, n * LANES : (n + 1) * LANES]
        layer_rows = []
        for ref in (gain1, gain2):
            for n in range(2):
                col = pl.multiple_of((lax.axis_index("fsdp") ^ p) * 2 * half + n * LANES, LANES)
                layer_rows.append(ref[pl.ds(0, 1), pl.ds(col, LANES)] if n < per else jnp.zeros((1, LANES), F32))
        block = jnp.concatenate(layer_rows + [small[pl.ds(4, 4), :], jnp.zeros((PAD - 8, LANES), F32)], axis=0)
        at = blocks * half
        out[pl.ds(at, PAD), :] = block.astype(BF)
        piece = parts[0].shape[0] // depths
        rows = pl.ds(p * piece, piece)
        total = parts[0][rows, :].astype(F32)
        for ref in parts[1:]:
            total = total + ref[rows, :].astype(F32)
        total = total.astype(BF)
        for n in range(total.shape[1] // LANES):
            out[pl.ds(at + PAD + n * piece, piece), :] = total[:, n * LANES : (n + 1) * LANES]


def projections_final_kernel(cfg, same, other, g_q, g_k, g_v, g_o, smalls):
    chips, width, half, piece = cfg
    core, chip, _ = place()
    model = g_q.shape[1]
    per = width // LANES
    blocks = 3 * per
    count = blocks * half + PAD + model // LANES * piece
    total = None
    for c in range(2):
        half_of = core if c == 0 else 1 - core
        row = pl.multiple_of(half_of * half, 16)
        for d in range(chips):
            value = (same if c == 0 else other)[pl.ds(d * count, count), :]
            for n, out in enumerate((g_q, g_k, g_v)):
                for m in range(per):
                    col = pl.multiple_of((chip ^ d) * width + m * LANES, LANES)
                    at = (n * per + m) * half
                    out[pl.ds(row, half), pl.ds(col, LANES)] = value[at : at + half].astype(F32)
            at = blocks * half
            small = value[at : at + PAD].astype(F32)
            total = small if total is None else total + small
            out_row = pl.multiple_of(half_of * half + (chip ^ d) * piece, 8)
            for n in range(model // LANES):
                start = at + PAD + n * piece
                g_o[pl.ds(out_row, piece), pl.ds(n * LANES, LANES)] = value[start : start + piece].astype(F32)
    smalls[...] = total


def w_out_kernel(cfg, same, other, out, full):
    chips, depths, piece = cfg
    core, chip, depth = place()
    here = 2 * chip + core
    rows_z = out.shape[0] // depths
    for c in range(2):
        for d in range(chips):
            value = (same if c == 0 else other)[pl.ds(d * depths * piece, depths * piece), :].astype(F32)
            for p in range(depths):
                row = (depth ^ p) * rows_z + (here ^ (2 * d + c)) * piece
                full[pl.ds(pl.multiple_of(row, 8), piece), :] = value[p * piece : (p + 1) * piece]
    out[...] = full[...].astype(BF)


def layer(
    chips, fsdp, inputs, time_ids, variate_ids, seq_lengths, w_query, w_key, w_value, w_out, w_gate,
    w_up, w_down, gain_attn, gain_ffn, head_bias, q_gain, k_gain, cotangent,
):
    _, slots, model = inputs.shape
    heads = model // HEAD_DIM // chips
    width = heads * HEAD_DIM
    rows_z = w_query.shape[0]
    half_z = rows_z // 2
    hidden = w_gate.shape[1]
    ff = hidden // chips
    ff_z = ff // fsdp
    ff_pad = -(-ff // 256) * 256
    chunk = 2 * slots
    span = chips * chunk
    core, chip, depth = lax.axis_index("core"), lax.axis_index("chip"), lax.axis_index("fsdp")
    here = 2 * chip + core
    heads_z, dims_z = head_bias.shape[0], q_gain.shape[0]
    last = []

    def step(kernel, cfg, out_shapes, *operands, after=(), **options):
        if cfg is not None:
            kernel = functools.partial(kernel, cfg)
        token = shape_of((8, LANES), F32)
        outs = kernel_call(kernel, out_shapes + [token], *operands, after=last[-1:] + list(after), **options)
        last.append(outs[-1])
        return outs[:-1]

    def pc(a):
        return lax.ppermute(a, "core", [(0, 1), (1, 0)])

    def pt(a, p):
        return lax.ppermute(a, "chip", [(n, n ^ p) for n in range(chips)])

    def pz(a, p):
        return lax.ppermute(a, "fsdp", [(n, n ^ p) for n in range(fsdp)])

    def stack(*parts, rows=None, after=()):
        counts = [rows or a.shape[0] for a in parts]
        out = shape_of((sum(counts), parts[0].shape[1]), BF)
        return step(stack_kernel, counts, [out], *[Far(a) for a in parts], us=0.6, after=after)[0]

    def gather_first(own):
        if chips == 4:
            return [own, pt(own, 1), pt(own, 2)]
        return [own] + [pt(own, d) for d in range(1, chips)]

    def gather_second(got):
        if chips != 4:
            return [[a] for a in got]
        rows, cols = got[0].shape
        cut = rows // 32 * 16
        first, second = step(
            cut_kernel, None, [shape_of((cut, cols), BF), shape_of((rows - cut, cols), BF)],
            Far(got[1]), Far(got[2]), us=0.8,
        )
        return [[a] for a in got] + [[pt(first, 2), pt(second, 1)]]

    def exchange(parts):
        return [parts[0]] + [pt(parts[d], d) for d in range(1, chips)]

    def scatter_layout(rows, axis):
        if chips != 4:
            return [(d, 0) for d in range(chips)], [rows] * chips
        cross = (1, 3) if axis == 1 else (2, 3)
        near = (0, 2) if axis == 1 else (0, 1)
        return [(1, cross.index(d) * rows) if d in cross else (0, near.index(d) * rows) for d in range(4)], [2 * rows] * 2

    def scatter_first(parts, axis):
        if chips != 4:
            return exchange(parts)
        return [parts[0], pt(parts[1], axis)]

    def scatter_second(got, axis):
        if chips != 4:
            return got
        rows, cols = got[0].shape
        own, send = step(half_sum_kernel, None, [shape_of((rows // 2, cols), BF)] * 2, *far(got), us=0.3)
        return [own, pt(send, 3 - axis)]

    def far(arrays):
        return [Far(a) for a in arrays]

    def joined(lists):
        return Far(*[a for part in lists for a in part])

    blocks = 3 * width // LANES
    body = blocks * half_z
    own_qkv = step(
        weight_kernel, width, [shape_of((body, LANES), BF)], Far(w_query), Far(w_key), Far(w_value), us=1.5
    )[0]
    packed_qkv = lax.all_gather(own_qkv, ("fsdp", "core"), axis=0, tiled=True)

    own_in, other_in = step(
        input_kernel, None, [shape_of((2 * slots + PAD, model), BF)] * 2,
        Far(inputs), time_ids, variate_ids, Far(cotangent), us=1.0,
    )
    got_in = pc(other_in)
    piece = rows_z // (2 * chips)
    own_small = step(
        small_kernel, None, [shape_of((PAD, LANES), BF)], gain_attn.reshape(-1, LANES),
        gain_ffn.reshape(-1, LANES), head_bias, q_gain[None], k_gain[None], us=0.6,
    )[0]
    got_small = [own_small] + [pz(own_small, p) for p in range(1, fsdp)]

    x_chunk = step(
        halves_kernel, 0, [shape_of((chunk + 2 * PAD, model), BF)], own_in, Far(got_in), us=1.0
    )[0]
    xs = gather_first(x_chunk)

    gu_blocks = -(-2 * ff // LANES)
    quarters = model // 2 // LANES
    padded = -(-ff_z // 16) * 16
    ff_piece = gu_blocks * half_z + quarters * padded
    own_ff = step(
        pack_kernel, (chips, fsdp, ff, ff_z), [shape_of((ff_piece, LANES), BF)],
        Far(w_gate), Far(w_up), Far(w_down), us=2.3,
    )[0]
    packed_ff = lax.all_gather(own_ff, ("fsdp", "core"), axis=0, tiled=True)

    params = step(params_kernel, fsdp, [shape_of((8, model), F32)], Far(*got_small), us=0.1)[0]
    xs = gather_second(xs)
    own_out = step(
        stack_kernel, [piece], [shape_of((piece, model), BF)],
        lax.dynamic_slice_in_dim(w_out, here * piece, piece, 0), us=0.1,
    )[0]
    z_out = step(
        layers_kernel, None, [shape_of((fsdp * piece, model), BF)],
        own_out, *[Far(pz(own_out, p)) for p in range(1, fsdp)], us=0.1,
    )[0]
    out_same = gather_first(z_out)

    n1, table, kinds, hots = step(
        norm_kernel, chips,
        [shape_of((span, model), BF), shape_of((span, LANES), F32)] + [shape_of((span, HEAD_DIM), BF)] * 2,
        joined(xs), jnp.asarray(turn_table(span)), params, scalars=seq_lengths, us=4.0, vmem=40,
    )
    out_same = gather_second(out_same)
    dy_chunk = step(halves_kernel, slots + PAD, [shape_of((chunk, model), BF)], own_in, Far(got_in), us=1.0)[0]
    dys = gather_first(dy_chunk)
    outs = step(
        attend_kernel, (chips, heads, fsdp),
        [Far(shape_of((span, width), BF))] * 3
        + [Far(shape_of((span, 2 * width), F32)), Far(shape_of((model, 3 * width), BF)), Far(shape_of((span, width), F32))]
        + [shape_of((chunk, width), BF)] * chips,
        Far(packed_qkv), Far(n1), Far(table), Far(kinds), Far(hots), params, us=FRONT_US, vmem=40,
    )
    q, k, v, pre, w_qkv, mix = outs[:6]
    mix_got = exchange(outs[6:])
    out_other = pc(stack(*[a for part in out_same for a in part], after=dys[1:]))
    w_o = step(
        w_out_kernel, (chips, fsdp, piece), [shape_of((model, model), BF)], joined(out_same), Far(out_other),
        us=1.5, scratch=[pltpu.VMEM((model, model), F32)],
    )[0]

    hidden_state, normed2 = step(
        functools.partial(mix_out_kernel, width), chips,
        [shape_of((chunk, model), F32), shape_of((chunk, model), BF)],
        Far(x_chunk), w_o, params, mix_got[0], *far(mix_got[1:]), us=2.2,
    )
    n2s = gather_first(normed2)
    dys = gather_second(dys)

    w_gu, w_d = step(
        unpack_kernel, (fsdp, ff, ff_z, ff_pad),
        [shape_of((model, 2 * ff_pad), BF), shape_of((ff_pad, model), BF)], Far(packed_ff), us=2.0,
    )

    def feed_forward(d):
        return step(
            ffn_kernel, (d, ff_pad),
            [shape_of((chunk, model), BF), shape_of((chunk, ff_pad), BF), shape_of((chunk, 2 * ff_pad), BF)],
            Far(*n2s[d]), Far(*dys[d]), w_gu, w_d, scalars=seq_lengths, us=3.3,
        )

    n2s_first, n2s = n2s, [[normed2]]
    ffn = [feed_forward(0)]
    n2s = gather_second(n2s_first)
    ffn += [feed_forward(d) for d in range(1, chips)]
    dn2_got = exchange([a[0] for a in ffn])

    packed_grad, gain2_part = step(
        ffn_grad_kernel, (chips, fsdp, ff, ff_z, ff_pad),
        [shape_of((2 * fsdp * ff_piece, LANES), BF), shape_of((8, model), F32)],
        joined(n2s), joined(dys), Far(*[a[1] for a in ffn]), Far(*[a[2] for a in ffn]), w_gu, params,
        scalars=seq_lengths, us=7.6, vmem=40,
    )
    ff_sum = lax.psum_scatter(packed_grad, ("fsdp", "core"), scatter_dimension=0, tiled=True)

    outs = step(
        functools.partial(hidden_back_kernel, width), chips,
        [shape_of((chunk, model), F32), shape_of((chunk, model), BF)] + [shape_of((chunk, width), BF)] * chips,
        hidden_state, Far(dy_chunk), params, w_o, dn2_got[0], *far(dn2_got[1:]), scalars=seq_lengths, us=2.2,
    )
    d_hidden, d_hidden_low = outs[:2]
    dmix_got = exchange(outs[2:])

    mine_o, theirs_o = step(
        out_grad_kernel, (chips, fsdp, width, piece), [shape_of((chips, fsdp, piece, model), BF)] * 2,
        d_hidden_low, *far(mix_got), us=2.2, scratch=[pltpu.VMEM((model, model), F32)],
    )
    got_o = pc(theirs_o)

    layout, rows = scatter_layout(fsdp * piece, 2)
    by_chip = step(
        core_sum_kernel, layout, [shape_of((n, model), BF) for n in rows], mine_o, Far(got_o), us=1.0
    )
    chip_o = scatter_first(by_chip, 2)
    layout, rows = scatter_layout(chunk, 1)
    downs = step(
        down_kernel, layout, [shape_of((n, model), BF) for n in rows], w_d, *[a[1] for a in ffn], us=1.8
    )
    down_got = scatter_first(downs, 1)

    d_qkv, small_part = step(
        attend_back_kernel, (chips, heads, width),
        [shape_of((span, 3 * width), BF), shape_of((8, LANES), F32)],
        Far(*dmix_got), *far((table, q, k, v, mix, pre)), params, us=BACK_US, vmem=40,
        scratch=[pltpu.VMEM((span, HEAD_DIM), BF)] * 2 + [pltpu.VMEM((span, width), F32)] * 3,
    )

    mine, theirs, gain1_part = step(
        qkv_grad_kernel, fsdp, [shape_of((fsdp * half_z, 3 * width), BF)] * 2 + [shape_of((8, model), F32)],
        Far(n1), d_qkv, Far(w_qkv), params, us=3.0, scratch=[pltpu.VMEM((model, 3 * width), F32)],
    )
    got = pc(theirs)
    chip_o = scatter_second(chip_o, 2)

    d_n1 = step(project_back_kernel, None, [shape_of((chunk, model), BF)] * chips, d_qkv, Far(w_qkv), us=2.0)
    dn1_got = exchange(d_n1)

    down_got = scatter_second(down_got, 1)
    count = body + PAD + model // LANES * piece
    messages = step(
        message_kernel, (fsdp, len(chip_o)), [shape_of((count, LANES), BF)] * fsdp,
        mine, Far(got), gain1_part, gain2_part, small_part, *far(chip_o), us=1.5,
    )
    z_got = [messages[0]] + [pz(messages[p], p) for p in range(1, fsdp)]

    ff_all = lax.all_gather(stack(ff_sum), ("chip", "core"), axis=0, tiled=True)
    own_result, their_result = step(
        output_kernel, len(down_got), [shape_of((slots, model), BF)] * 2,
        Far(hidden_state), *far(down_got), scalars=seq_lengths, us=1.8,
    )
    got_result = pc(their_result)
    z_sum = step(sum_kernel, None, [shape_of((count, LANES), BF)], z_got[0], *far(z_got[1:]), us=1.0)[0]
    same = gather_first(z_sum)

    own_grad, their_grad = step(
        input_back_kernel, chips, [shape_of((slots, model), F32), shape_of((slots, model), BF)],
        Far(x_chunk), Far(d_hidden), params, dn1_got[0], *far(dn1_got[1:]), us=1.8,
    )
    got_grad = pc(their_grad)
    same = gather_second(same)
    other = pc(stack(*[a for part in same for a in part]))
    grad_gate, grad_up, grad_down = step(
        ffn_final_kernel, (chips, fsdp, ff, ff_z),
        [shape_of((rows_z, hidden), F32)] * 2 + [shape_of((hidden // fsdp, model), F32)], Far(ff_all), us=5.0,
    )
    grad_query, grad_key, grad_value, grad_out, small_sum = step(
        projections_final_kernel, (chips, width, half_z, piece),
        [shape_of((rows_z, model), F32)] * 4 + [shape_of((PAD, LANES), F32)], joined(same), Far(other), us=3.0,
    )
    output, grad_inputs = step(
        by_sequence_kernel, None, [shape_of((2, slots, model), BF), shape_of((2, slots, model), F32)],
        own_result, Far(got_result), own_grad, Far(got_grad), us=1.0,
    )
    per = rows_z // LANES
    grad_bias = lax.dynamic_slice(small_sum, (SAME_ROW, depth * heads_z), (2, heads_z)).T
    grad_q_gain = lax.dynamic_slice(small_sum, (Q_ROW, depth * dims_z), (1, dims_z))[0]
    grad_k_gain = lax.dynamic_slice(small_sum, (K_ROW, depth * dims_z), (1, dims_z))[0]
    return (
        output, grad_inputs, grad_query, grad_key, grad_value, grad_out, grad_gate, grad_up, grad_down,
        small_sum[:per].reshape(-1), small_sum[2 : 2 + per].reshape(-1), grad_bias, grad_q_gain, grad_k_gain,
    )


def solution(mesh):
    ctx, fsdp = mesh.shape["ctx"], mesh.shape["fsdp"]
    chips = ctx // 2
    split = Mesh(mesh.devices.reshape(chips, 2, fsdp), ("chip", "core", "fsdp"))
    rows, row = P("fsdp", None), P("fsdp")
    block, ids = P("fsdp", ("chip", "core"), None), P("fsdp", ("chip", "core"))
    return jax.shard_map(
        functools.partial(layer, chips, fsdp),
        mesh=split,
        in_specs=(block, ids, ids, row) + (rows,) * 7 + (row, row, rows, row, row, block),
        out_specs=(block, block) + (rows,) * 7 + (row, row, rows, row, row),
        check_vma=False,
    )
```
